512 devices in a mesh: ctx: 128 (over z, y_lo, x), head: 4 (over y_hi, core).
Axes of the slice: x: 4, y: 4 (y_hi: 2, y_lo: 2; y = y_hi * 2 + y_lo), z: 16, core: 2. Of those that a mesh axis runs over, the one named last changes fastest.
Arguments:
- cache_latent: bfloat16 [2, 32768, 576], P(None, 'ctx'), may hold values from -8 to 8
- group_latent: bfloat16 [2, 1024, 576], P(None, 'ctx'), may hold values from -8 to 8
- group_query: bfloat16 [2, 1024, 3072], P(None, 'ctx', 'head'), may hold values from -8 to 8
- decode_query: bfloat16 [2, 2, 8, 3072], P(None, None, None, 'head'), may hold values from -8 to 8
- group_start: int32 [2], replicated, may hold values from 16384 to 32768, as said below
- w_key: bfloat16 [512, 2048], P(None, 'head'), may hold values from -0.25 to 0.25
- w_value: bfloat16 [512, 2048], P(None, 'head'), may hold values from -0.25 to 0.25
- w_out: bfloat16 [2048, 2048], P('head'), may hold values from -0.125 to 0.125
Outputs:
- group_hidden: bfloat16 [2, 1024, 2048], P(None, 'ctx', 'head')
- decode_hidden: bfloat16 [2, 2, 8, 2048], P(None, None, None, 'head')
The draws below stay inside these ranges and needn't reach their ends.
Inputs may be any that keep to these rules, and one draw needn't show every extreme that they name: Cache positions below group_start[b] hold request b's context; in every draw exactly one request has 32768, every other fewer.
All inputs are finite; a program needn't handle non-finite values.
Results may differ from the reference program's by a relative error of at most 0.015.
Values may be sent and summed in bfloat16 or wider, within the bound.
A program may use at most 64 MiB of HBM per device.

```python
import jax
import jax.numpy as jnp
from jax import lax

D_LAT = 512
D_ROPE = 64
D_NOPE = 128
D_V = 128
HEADS = 16
HID = 2048
REQS = 2
DRAFT = 8
STEPS = 2
CACHE = 32768
GROUP = 1024


def draw_cache_latent(key, part):
    key = jax.random.fold_in(key, 11)
    base_key = jax.random.fold_in(key, 0)
    shape_all = (REQS, CACHE, D_LAT + D_ROPE)
    values = jnp.clip(jax.random.normal(base_key, shape_all, jnp.float32), -8.0, 8.0)
    return values.astype(jnp.bfloat16)


def draw_group_latent(key, part):
    key = jax.random.fold_in(key, 13)
    base_key = jax.random.fold_in(key, 0)
    shape_all = (REQS, GROUP, D_LAT + D_ROPE)
    values = jnp.clip(jax.random.normal(base_key, shape_all, jnp.float32), -8.0, 8.0)
    return values.astype(jnp.bfloat16)


def draw_group_query(key, part):
    key = jax.random.fold_in(key, 23)
    base_key = jax.random.fold_in(key, 0)
    shape_all = (REQS, GROUP, HEADS, D_NOPE + D_ROPE)
    values = jnp.clip(2.0 * jax.random.normal(base_key, shape_all, jnp.float32), -8.0, 8.0)
    return values.reshape(REQS, GROUP, HEADS * (D_NOPE + D_ROPE)).astype(jnp.bfloat16)


def draw_decode_query(key, part):
    key = jax.random.fold_in(key, 29)
    base_key = jax.random.fold_in(key, 0)
    shape_all = (STEPS * REQS, DRAFT, HEADS, D_NOPE + D_ROPE)
    values = jnp.clip(3.0 * jax.random.normal(base_key, shape_all, jnp.float32), -8.0, 8.0)
    return values.reshape(STEPS, REQS, DRAFT, HEADS * (D_NOPE + D_ROPE)).astype(jnp.bfloat16)


def draw_group_start(key, part):
    key = jax.random.fold_in(key, 37)
    first_key, pick_key = jax.random.split(key, 2)
    starts = jax.random.randint(first_key, (REQS,), CACHE // 2, CACHE)
    chosen = jax.random.randint(pick_key, (), 0, REQS)
    return jnp.where(jnp.arange(REQS) == chosen, CACHE, starts).astype(jnp.int32)


def levels(stream_key, dims, shards, low, largest):
    def one(axis_at, parts):
        heights = jax.random.uniform(jax.random.fold_in(jax.random.fold_in(stream_key, 6), axis_at), (parts,), jnp.float32, low / len(shards), largest / len(shards))
        return jnp.repeat(jnp.exp(heights), dims[axis_at] // parts).reshape((-1,) + (1,) * (len(dims) - axis_at - 1))

    factor_of = one(*shards[0])
    for cut in shards[1:]:
        factor_of = factor_of * one(*cut)
    return factor_of


def gaussian(key, dims, width, bound, cuts=(), held_as=jnp.bfloat16):
    gain = levels(key, dims, cuts, -0.22, 0.18) if cuts else 1.0
    values = jax.random.normal(key, dims, jnp.float32) * width * gain
    return jnp.minimum(jnp.maximum(values, -bound), bound).astype(held_as)


def setup_inputs(seed: int = 0) -> dict:
    seeds = jax.random.split(jax.random.key(seed), 9)
    return {
        "cache_latent": draw_cache_latent(jax.random.fold_in(seeds[8], 71), 0),
        "group_latent": draw_group_latent(jax.random.fold_in(seeds[8], 71), 0),
        "group_query": draw_group_query(jax.random.fold_in(seeds[8], 71), 0),
        "decode_query": draw_decode_query(jax.random.fold_in(seeds[8], 71), 0),
        "group_start": draw_group_start(jax.random.fold_in(seeds[8], 71), 0),
        "w_key": gaussian(seeds[5], (D_LAT, HEADS * D_NOPE), D_LAT ** -0.5, 0.25, ((1, 4),)),
        "w_value": gaussian(seeds[6], (D_LAT, HEADS * D_V), D_LAT ** -0.5, 0.25, ((1, 4),)),
        "w_out": gaussian(seeds[7], (HEADS * D_V, HID), (HEADS * D_V) ** -0.5, 0.125, ((0, 4),)),
    }


def group_request(latent, queries, w_key, w_value):
    wide = D_NOPE + D_ROPE
    score_scale = 1.0 / (wide ** 0.5)
    key_rows = jnp.dot(latent[:, :D_LAT], w_key, preferred_element_type=jnp.float32).astype(jnp.bfloat16)
    value_rows = jnp.dot(latent[:, :D_LAT], w_value, preferred_element_type=jnp.float32).astype(jnp.bfloat16)
    key_rows = key_rows.reshape(GROUP, HEADS, D_NOPE).transpose(1, 0, 2)
    value_rows = value_rows.reshape(GROUP, HEADS, D_V).transpose(1, 0, 2)
    by_head = queries.reshape(GROUP, HEADS, wide).transpose(1, 0, 2)
    rope_part = latent[:, D_LAT:]
    causal = jnp.arange(GROUP, dtype=jnp.int32)[None, :] <= jnp.arange(GROUP, dtype=jnp.int32)[:, None]

    def one_head(pieces):
        head_query, head_keys, head_values = pieces
        scores = jnp.dot(head_query[:, :D_NOPE], head_keys.T, preferred_element_type=jnp.float32)
        scores = scores + jnp.dot(head_query[:, D_NOPE:], rope_part.T, preferred_element_type=jnp.float32)
        scores = jnp.where(causal, scores * score_scale, -jnp.inf)
        row_peak = jnp.max(scores, axis=1, keepdims=True)
        weights = jnp.exp(scores - row_peak)
        row_total = jnp.sum(weights, axis=1, keepdims=True)
        mixture = jnp.dot(weights.astype(jnp.bfloat16), head_values, preferred_element_type=jnp.float32)
        return (mixture / row_total).astype(jnp.bfloat16)

    result = lax.map(one_head, (by_head, key_rows, value_rows))
    return result.transpose(1, 0, 2).reshape(GROUP, HEADS * D_V)


def decode_rows(queries, key_all, key_valid, w_key, w_value):
    wide = D_NOPE + D_ROPE
    score_scale = 1.0 / (wide ** 0.5)
    by_head = queries.reshape(DRAFT, HEADS, wide)
    absorbed = jnp.einsum('qhd,chd->qhc', by_head[..., :D_NOPE].astype(jnp.float32),
                          w_key.reshape(D_LAT, HEADS, D_NOPE).astype(jnp.float32),
                          precision=lax.Precision.HIGHEST).astype(jnp.bfloat16)
    flat_rows = absorbed.reshape(DRAFT * HEADS, D_LAT)
    rope_rows = by_head[..., D_NOPE:].reshape(DRAFT * HEADS, D_ROPE)
    scores = jnp.dot(flat_rows, key_all[:, :D_LAT].T, preferred_element_type=jnp.float32)
    scores = scores + jnp.dot(rope_rows, key_all[:, D_LAT:].T, preferred_element_type=jnp.float32)
    scores = jnp.where(key_valid[None, :], scores * score_scale, -jnp.inf)
    row_peak = jnp.max(scores, axis=1, keepdims=True)
    weights = jnp.exp(scores - row_peak)
    row_total = jnp.sum(weights, axis=1, keepdims=True)
    latent_out = jnp.dot(weights.astype(jnp.bfloat16), key_all[:, :D_LAT], preferred_element_type=jnp.float32) / row_total
    latent_out = latent_out.reshape(DRAFT, HEADS, D_LAT)
    attention = jnp.einsum('qhc,chd->qhd', latent_out, w_value.reshape(D_LAT, HEADS, D_V).astype(jnp.float32),
                           precision=lax.Precision.HIGHEST).astype(jnp.bfloat16)
    return attention.reshape(DRAFT, HEADS * D_V)


def reference(cache_latent, group_latent, group_query, decode_query, group_start, w_key, w_value, w_out):
    group_attention = lax.map(lambda pieces: group_request(pieces[0], pieces[1], w_key, w_value),
                              (group_latent, group_query))
    group_hidden = jnp.dot(group_attention.reshape(REQS * GROUP, HEADS * D_V), w_out,
                           preferred_element_type=jnp.float32).astype(jnp.bfloat16).reshape(REQS, GROUP, HID)
    positions = jnp.arange(CACHE + GROUP, dtype=jnp.int32)

    def request_decode(pieces):
        cache_rows, group_rows, first_pos, step_queries = pieces
        key_all = jnp.concatenate([cache_rows, group_rows], axis=0)
        key_valid = (positions < first_pos) | (positions >= CACHE)
        return lax.map(lambda queries: decode_rows(queries, key_all, key_valid, w_key, w_value), step_queries)

    decoded = lax.map(request_decode, (cache_latent, group_latent, group_start, decode_query.transpose(1, 0, 2, 3)))
    decoded = decoded.transpose(1, 0, 2, 3)
    decode_hidden = jnp.dot(decoded.reshape(STEPS * REQS * DRAFT, HEADS * D_V), w_out,
                            preferred_element_type=jnp.float32).astype(jnp.bfloat16).reshape(STEPS, REQS, DRAFT, HID)
    return (group_hidden, decode_hidden)
```

```python
import jax
import jax.numpy as jnp
from jax import lax
from jax.experimental import pallas as pl
from jax.experimental.pallas import tpu as pltpu
from jax.sharding import PartitionSpec as P

MESH = pl.DeviceIdType.MESH
BF = jnp.bfloat16
F32 = jnp.float32
LAT = 512
ROPE = 64
NOPE = 128
WIDE = NOPE + ROPE
HALF = 384
LOCAL = 4
NZ = 16
NXY = 8
SCALE = 1.0 / WIDE**0.5
LOW = -1e30


def dot(a, b):
    return lax.dot_general(a, b, (((1,), (0,)), ((), ())), preferred_element_type=F32)


def dot_t(a, b):
    return lax.dot_general(a, b, (((1,), (1,)), ((), ())), preferred_element_type=F32)


def iota(shape, axis):
    return lax.broadcasted_iota(jnp.int32, shape, axis)


def split(value, pieces):
    out = []
    for _ in range(pieces):
        head = value.astype(BF).astype(F32)
        out.append(head)
        value = value - head
    return out


def by_lane(shape, columns):
    lane = iota(shape, 1)
    tile = jnp.zeros(shape, F32)
    for at, column in columns.items():
        tile = jnp.where(lane == at, column, tile)
    return tile


def merge(stats, at, blocks):
    peak = stats[..., at : at + 1] + stats[..., at + 1 : at + 2] + stats[..., at + 2 : at + 3]
    total = stats[..., at + 3 : at + 4] + stats[..., at + 4 : at + 5]
    top = jnp.max(peak, axis=0, keepdims=True)
    factor = jnp.exp(peak - top)
    return top[0], jnp.sum(factor * total, axis=0), jnp.sum(factor * blocks, axis=0)


def kernel(
    start_ref, cache_hbm, glat_hbm, gq_hbm, dq_hbm, wk_hbm, wv_hbm, wo_hbm,
    group_out, decode_out,
    cache, glat, gq, dq, wk, wv, wo,
    keys, queries, big_q, dsend, drecv, zrecv, psend, precv, gsend, grecv, hsend, hrecv,
    local_sem, send_sem, recv_sem,
):
    ctx = lax.axis_index("ctx")
    head = lax.axis_index("head")
    z = ctx // NXY
    xy = ctx % NXY
    yl = xy // 4
    x = xy % 4
    core = head % 2
    sibling = head // 2 * 2 + (1 - core)

    def xy_device(rel):
        dy, dx = rel // 4, rel % 4
        return z * NXY + (yl + dy) % 2 * 4 + (x + dx) % 4

    def back(rel):
        return rel // 4 * 4 + (4 - rel % 4) % 4

    def z_device(d):
        return (z + d + NZ) % NZ * NXY + xy

    def absolute(rel):
        return (yl + rel // 4) % 2 * 4 + (x + rel % 4) % 4

    def remote(src, dst, phase, device):
        pltpu.make_async_remote_copy(
            src_ref=src, dst_ref=dst, send_sem=send_sem.at[phase], recv_sem=recv_sem.at[phase],
            device_id=device, device_id_type=MESH,
        ).start()

    def took(ref, sem):
        pltpu.make_async_copy(ref, ref, sem).wait()

    loads = {}
    for at, (name, src, dst) in enumerate((
        ("glat", glat_hbm, glat), ("gq", gq_hbm, gq), ("dq", dq_hbm, dq), ("wk", wk_hbm, wk),
        ("cache", cache_hbm, cache), ("wv", wv_hbm, wv), ("wo", wo_hbm, wo),
    )):
        loads[name] = pltpu.make_async_copy(src, dst, local_sem.at[at])
        loads[name].start()
    barrier = pltpu.get_barrier_semaphore()

    def greet(device):
        pl.semaphore_signal(barrier, inc=1, device_id=device, device_id_type=MESH)

    for d in (4, 3, 2, 1):
        greet((z_device(d), head))
        greet((z_device(-d), head))
    for rel in range(1, NXY):
        greet((xy_device(rel), head))
    for rel in range(1, 4):
        greet((ctx, (head + rel) % 4))

    loads["glat"].wait()
    own = glat[...].astype(F32).reshape(16, LAT + ROPE).astype(BF)
    keys[0, 8] = own[:, :HALF]
    keys[1, 8] = jnp.concatenate(
        [own[:, HALF:], jnp.zeros((16, 2 * HALF - LAT - ROPE), BF)], axis=1
    )
    loads["gq"].wait()
    queries[0] = gq[...].astype(F32).reshape(16, LOCAL * WIDE).astype(BF)

    loads["dq"].wait()
    rows = NXY * 16
    flat = dq[...].astype(F32).reshape(32, LOCAL * WIDE).astype(BF)
    row = iota((rows, 32), 0)
    pick = absolute(row // 16) * 4 + row % 4 == iota((rows, 32), 1)
    spread = dot(jnp.where(pick, 1.0, 0.0).astype(BF), flat)
    row = iota((rows, 1), 0)
    row_head = row // 4 % 4
    row_req = absolute(row // 16) // 2 % 2
    nope = jnp.concatenate(
        [
            jnp.where(row_head == h, spread[:, h * WIDE : h * WIDE + NOPE], 0.0)
            for h in range(LOCAL)
        ],
        axis=1,
    ).astype(BF)
    rope = jnp.zeros((rows, ROPE), F32)
    for h in range(LOCAL):
        rope = jnp.where(row_head == h, spread[:, h * WIDE + NOPE : (h + 1) * WIDE], rope)
    rope = rope.astype(BF)
    loads["wk"].wait()
    absorbed = dot_t(nope, wk[...]).astype(BF)

    pl.semaphore_wait(barrier, 18)
    for d in (4, 3, 2, 1):
        remote(keys.at[core, 8], keys.at[core, 8 - d], 0, (z_device(d), head))
        remote(keys.at[core, 8], keys.at[core, 8 + d], 1, (z_device(-d), head))
    for rel in range(NXY - 1, 0, -1):
        remote(queries.at[0], queries.at[back(rel)], 2, (xy_device(rel), head))

    loads["cache"].wait()
    scores = []
    masks = []
    for r in range(2):
        got = dot_t(absorbed, cache[r, :, :LAT]) + dot_t(rope, cache[r, :, LAT:])
        position = ctx * 256 + iota((1, 256), 1)
        allowed = (position < start_ref[r]) & (row_req == r)
        masks.append(allowed)
        scores.append(jnp.where(allowed, got * SCALE, LOW))
    got = dot_t(absorbed, own[:, :LAT]) + dot_t(rope, own[:, LAT:])
    allowed = iota((1, 16), 1) // 8 == row_req
    masks.append(allowed)
    scores.append(jnp.where(allowed, got * SCALE, LOW))
    peak = jnp.max(scores[0], axis=1, keepdims=True)
    for got in scores[1:]:
        peak = jnp.maximum(peak, jnp.max(got, axis=1, keepdims=True))
    total = jnp.zeros((rows, 1), F32)
    mixture = jnp.zeros((rows, LAT), F32)
    for got, allowed, latent in zip(
        scores, masks, (cache[0, :, :LAT], cache[1, :, :LAT], own[:, :LAT])
    ):
        weights = jnp.where(allowed, jnp.exp(got - peak), 0.0)
        total = total + jnp.sum(weights, axis=1, keepdims=True)
        mixture = mixture + dot(weights.astype(BF), latent)
    loads["wv"].wait()
    wide = dot(mixture.astype(BF), wv[...])
    part = jnp.zeros((rows, NOPE), F32)
    for h in range(LOCAL):
        part = jnp.where(row_head == h, wide[:, h * 128 : (h + 1) * 128], part)
    stats = by_lane((rows, 128), dict(enumerate(split(peak, 3) + split(total, 2))))
    packed = jnp.concatenate([part, stats], axis=1).astype(BF).reshape(NXY, 16, 256)
    dsend[...] = packed
    drecv[0] = packed[0]
    for rel in range(NXY - 1, 0, -1):
        remote(dsend.at[rel], drecv.at[back(rel)], 3, (xy_device(rel), head))

    took(queries.at[1:NXY], recv_sem.at[2])
    all_q = queries[...].reshape(128, LOCAL * WIDE)
    for h in range(LOCAL):
        block = dot_t(all_q[:, h * WIDE : h * WIDE + NOPE], wk[:, h * 128 : (h + 1) * 128])
        big_q[h * 128 : (h + 1) * 128, :LAT] = block.astype(BF)
        big_q[h * 128 : (h + 1) * 128, LAT:] = jnp.concatenate(
            [
                all_q[:, h * WIDE + NOPE : (h + 1) * WIDE],
                jnp.zeros((128, 2 * HALF - LAT - ROPE), BF),
            ],
            axis=1,
        )

    took(keys.at[0, 4:8], recv_sem.at[0])
    took(keys.at[0, 9:13], recv_sem.at[1])
    remote(keys.at[core, 4:8], keys.at[core, 0:4], 4, (z_device(4), head))
    remote(keys.at[core, 9:12], keys.at[core, 13:16], 5, (z_device(-4), head))
    remote(keys.at[core, 4:8], keys.at[core, 4:8], 6, (ctx, sibling))
    remote(keys.at[core, 9:13], keys.at[core, 9:13], 7, (ctx, sibling))

    took(drecv.at[1:NXY], recv_sem.at[3])
    packed = drecv[...].astype(F32)
    peak, total, part = merge(packed[..., 128:], 0, packed[..., :128])
    stats = by_lane((16, 128), dict(enumerate(split(peak, 3) + split(total, 2))))
    zrecv[0] = jnp.concatenate([part, stats], axis=1).astype(BF)

    def send_z(j, carry):
        d = 8 + (j % 2 * 2 - 1) * ((j + 1) // 2)
        remote(zrecv.at[0], zrecv.at[NZ - d], 8, (z_device(d), head))
        return carry

    lax.fori_loop(0, NZ - 1, send_z, 0)

    took(keys.at[0, 0:4], recv_sem.at[4])
    took(keys.at[0, 13:16], recv_sem.at[5])
    remote(keys.at[core, 0:4], keys.at[core, 0:4], 9, (ctx, sibling))
    remote(keys.at[core, 13:16], keys.at[core, 13:16], 10, (ctx, sibling))
    took(keys.at[0, 4:8], recv_sem.at[6])
    took(keys.at[0, 9:13], recv_sem.at[7])
    took(keys.at[0, 0:4], recv_sem.at[9])
    took(keys.at[0, 13:16], recv_sem.at[10])

    first = keys[0].reshape(256, HALF)
    second = keys[1].reshape(256, HALF)
    scores = dot_t(big_q[:, :HALF], first) + dot_t(big_q[:, HALF:], second)
    row = iota((LOCAL * 128, 1), 0)
    col = iota((1, 256), 1)
    query_at = (z * NXY + absolute(row // 16 % NXY)) * 8 + row % 8
    key_at = ((z + col // 16 + 8) % NZ * NXY + xy) * 8 + col % 8
    allowed = (key_at <= query_at) & (row // 8 % 2 == col // 8 % 2)
    scores = jnp.where(allowed, scores * SCALE, LOW)
    peak = jnp.max(scores, axis=1, keepdims=True)
    weights = jnp.where(allowed, jnp.exp(scores - peak), 0.0)
    total = jnp.sum(weights, axis=1, keepdims=True)
    weights = weights.astype(BF)
    mixture = jnp.concatenate(
        [dot(weights, first), dot(weights, second[:, : LAT - HALF])], axis=1
    ).astype(BF)
    columns = {}
    for h in range(LOCAL):
        at = slice(h * 128, (h + 1) * 128)
        part = dot(mixture[at], wv[:, at]).astype(BF).reshape(NXY, 16, 128)
        gsend[:, :, at] = part
        grecv[0, :, at] = part[0]
        for k, column in enumerate(split(peak[at], 3) + split(total[at], 2)):
            columns[8 * h + k] = column
    stats = by_lane((128, 128), columns).astype(BF).reshape(NXY, 16, 128)
    gsend[:, :, LAT:] = stats
    grecv[0, :, LAT:] = stats[0]
    for rel in range(NXY - 1, 0, -1):
        remote(gsend.at[rel], grecv.at[back(rel)], 11, (xy_device(rel), head))

    took(zrecv.at[1:NZ], recv_sem.at[8])
    packed = zrecv[...].astype(F32)
    peak, total, part = merge(packed[..., 128:], 0, packed[..., :128])
    attention = (part / total).astype(BF)
    row = iota((64, 16), 0)
    pick = row // 16 * 4 + row % 4 == iota((64, 16), 1)
    spread = dot(jnp.where(pick, 1.0, 0.0).astype(BF), attention).astype(BF)
    lined = jnp.concatenate([spread[h * 16 : (h + 1) * 16] for h in range(LOCAL)], axis=1)
    loads["wo"].wait()
    hidden = dot(lined, wo[...])
    block = iota((16, 128), 0) // 4
    for j in range(4):
        tile = jnp.zeros((16, 128), F32)
        for c in range(4):
            at = j * 512 + c * 128
            tile = jnp.where(block == c, hidden[:, at : at + 128], tile)
        psend[j] = tile.astype(BF)
    precv[0] = psend[head]

    def send_plane(j, carry):
        k = 31 - j
        rel, turn = k // 4, k % 4
        there = (head + turn) % 4
        slot = back(rel) * 4 + (4 - turn) % 4
        remote(psend.at[there], precv.at[slot], 12, (xy_device(rel), there))
        return carry

    lax.fori_loop(0, 31, send_plane, 0)

    took(grecv.at[1:NXY], recv_sem.at[11])
    stats = grecv[:, :, LAT:].astype(F32)
    blocks = []
    for h in range(LOCAL):
        got = grecv[:, :, h * 128 : (h + 1) * 128].astype(F32)
        peak, total, part = merge(stats, 8 * h, got)
        blocks.append((part / total).astype(BF))
    hidden = dot(jnp.concatenate(blocks, axis=1), wo[...]).astype(BF)
    for j in range(4):
        hsend[j] = hidden[:, j * 512 : (j + 1) * 512]
    hrecv[0] = hsend[head]
    for turn in (2, 3, 1):
        there = (head + turn) % 4
        remote(hsend.at[there], hrecv.at[4 - turn], 13, (ctx, there))

    took(precv.at[1:32], recv_sem.at[12])
    summed = jnp.sum(precv[...].astype(F32).reshape(NXY, 4, 16, 128), axis=1)
    summed = summed.reshape(128, 128).astype(BF)
    row = iota((128, 128), 0)
    col = iota((128, 128), 1)
    pick = (row // 32 == col // 4 % 4) & (row % 32 == absolute(col // 16) * 4 + col % 4)
    placed = dot(jnp.where(pick, 1.0, 0.0).astype(BF), summed)
    decode_out[...] = (
        jnp.concatenate([placed[c * 32 : (c + 1) * 32] for c in range(4)], axis=1)
        .reshape(2, 2, 8, 512)
        .astype(BF)
    )
    took(hrecv.at[1:4], recv_sem.at[13])
    group_out[...] = (
        jnp.sum(hrecv[...].astype(F32), axis=0).reshape(2, 8, 512).astype(BF)
    )

    for phase, ref in (
        (0, keys.at[0, 4:8]), (1, keys.at[0, 9:13]), (2, queries.at[1:NXY]), (3, drecv.at[1:NXY]),
        (4, keys.at[0, 0:4]), (5, keys.at[0, 13:16]), (6, keys.at[0, 4:8]), (7, keys.at[0, 9:13]),
        (8, zrecv.at[1:NZ]), (9, keys.at[0, 0:4]), (10, keys.at[0, 13:16]),
        (11, grecv.at[1:NXY]), (12, precv.at[1:32]), (13, hrecv.at[1:4]),
    ):
        took(ref, send_sem.at[phase])


def shards(
    cache_latent, group_latent, group_query, decode_query, group_start, w_key, w_value, w_out
):
    anywhere = pl.BlockSpec(memory_space=pl.ANY)
    vmem = pl.BlockSpec(memory_space=pltpu.VMEM)
    return pl.pallas_call(
        kernel,
        out_shape=(
            jax.ShapeDtypeStruct((2, 8, 512), BF),
            jax.ShapeDtypeStruct((2, 2, 8, 512), BF),
        ),
        in_specs=[pl.BlockSpec(memory_space=pltpu.SMEM)] + [anywhere] * 7,
        out_specs=(vmem, vmem),
        scratch_shapes=[
            pltpu.VMEM((2, 256, 576), BF),
            pltpu.VMEM((2, 8, 576), BF),
            pltpu.VMEM((2, 8, 768), BF),
            pltpu.VMEM((2, 2, 8, 768), BF),
            pltpu.VMEM((512, 512), BF),
            pltpu.VMEM((512, 512), BF),
            pltpu.VMEM((512, 2048), BF),
            pltpu.VMEM((2, NZ, 16, HALF), BF),
            pltpu.VMEM((NXY, 16, 768), BF),
            pltpu.VMEM((512, 2 * HALF), BF),
            pltpu.VMEM((NXY, 16, 256), BF),
            pltpu.VMEM((NXY, 16, 256), BF),
            pltpu.VMEM((NZ, 16, 256), BF),
            pltpu.VMEM((4, 16, 128), BF),
            pltpu.VMEM((32, 16, 128), BF),
            pltpu.VMEM((NXY, 16, 640), BF),
            pltpu.VMEM((NXY, 16, 640), BF),
            pltpu.VMEM((4, 16, 512), BF),
            pltpu.VMEM((4, 16, 512), BF),
            pltpu.SemaphoreType.DMA((7,)),
            pltpu.SemaphoreType.DMA((14,)),
            pltpu.SemaphoreType.DMA((14,)),
        ],
        compiler_params=pltpu.CompilerParams(
            collective_id=0, has_side_effects=True, vmem_limit_bytes=32 << 20
        ),
        name="latent_attention",
    )(
        group_start, cache_latent, group_latent, group_query, decode_query, w_key, w_value, w_out
    )


def solution(mesh):
    in_specs = (
        P(None, "ctx", None),
        P(None, "ctx", None),
        P(None, "ctx", "head"),
        P(None, None, None, "head"),
        P(),
        P(None, "head"),
        P(None, "head"),
        P("head", None),
    )
    out_specs = (P(None, "ctx", "head"), P(None, None, None, "head"))
    return jax.shard_map(shards, mesh=mesh, in_specs=in_specs, out_specs=out_specs, check_vma=False)
```

```python
import jax
import jax.numpy as jnp
from jax import lax
from jax.experimental import pallas as pl
from jax.experimental.pallas import tpu as pltpu
from jax.sharding import PartitionSpec as P

MESH = pl.DeviceIdType.MESH
BF = jnp.bfloat16
F32 = jnp.float32
LAT = 512
ROPE = 64
NOPE = 128
WIDE = NOPE + ROPE
HALF = 384
LOCAL = 4
NZ = 16
NXY = 8
SCALE = 1.0 / WIDE**0.5
LOW = -1e30


def dot(a, b):
    return lax.dot_general(a, b, (((1,), (0,)), ((), ())), preferred_element_type=F32)


def dot_t(a, b):
    return lax.dot_general(a, b, (((1,), (1,)), ((), ())), preferred_element_type=F32)


def iota(shape, axis):
    return lax.broadcasted_iota(jnp.int32, shape, axis)


def split(value, pieces):
    out = []
    for _ in range(pieces):
        head = value.astype(BF).astype(F32)
        out.append(head)
        value = value - head
    return out


def by_lane(shape, columns):
    lane = iota(shape, 1)
    tile = jnp.zeros(shape, F32)
    for at, column in columns.items():
        tile = jnp.where(lane == at, column, tile)
    return tile


def merge(stats, at, blocks):
    peak = stats[..., at : at + 1] + stats[..., at + 1 : at + 2] + stats[..., at + 2 : at + 3]
    total = stats[..., at + 3 : at + 4] + stats[..., at + 4 : at + 5]
    top = jnp.max(peak, axis=0, keepdims=True)
    factor = jnp.exp(peak - top)
    return top[0], jnp.sum(factor * total, axis=0), jnp.sum(factor * blocks, axis=0)


def kernel(
    start_hbm, cache_hbm, glat_hbm, gq_hbm, dq_hbm, wk_hbm, wv_hbm, wo_hbm,
    group_out, decode_out,
    start, cache, glat, gq, dq, wk, wv, wo,
    keys, queries, big_q, dsend, drecv, zrecv, psend, precv, gsend, grecv, hsend, hrecv,
    local_sem, send_sem, recv_sem, key_send, key_recv, here,
):
    ctx = lax.axis_index("ctx")
    head = lax.axis_index("head")
    z = ctx // NXY
    xy = ctx % NXY
    yl = xy // 4
    x = xy % 4
    core = head % 2
    sibling = head // 2 * 2 + (1 - core)

    def xy_device(rel):
        dy, dx = rel // 4, rel % 4
        return z * NXY + (yl + dy) % 2 * 4 + (x + dx) % 4

    def back(rel):
        return rel // 4 * 4 + (4 - rel % 4) % 4

    def z_device(d):
        return (z + d) % NZ * NXY + xy

    def absolute(rel):
        return (yl + rel // 4) % 2 * 4 + (x + rel % 4) % 4

    def remote(src, dst, phase, device):
        pltpu.make_async_remote_copy(
            src_ref=src, dst_ref=dst, send_sem=send_sem.at[phase], recv_sem=recv_sem.at[phase],
            device_id=device, device_id_type=MESH,
        ).start()

    def took(ref, sem):
        pltpu.make_async_copy(ref, ref, sem).wait()

    loads = {}
    for at, (name, src, dst) in enumerate((
        ("glat", glat_hbm, glat), ("gq", gq_hbm, gq), ("dq", dq_hbm, dq), ("wk", wk_hbm, wk),
        ("start", start_hbm, start), ("cache", cache_hbm, cache), ("wv", wv_hbm, wv),
        ("wo", wo_hbm, wo),
    )):
        loads[name] = pltpu.make_async_copy(src, dst, local_sem.at[at])
        loads[name].start()
    keys[...] = jnp.zeros_like(keys)
    barrier = pltpu.get_barrier_semaphore()

    def greet(device):
        pl.semaphore_signal(barrier, inc=1, device_id=device, device_id_type=MESH)

    def ranked(r):
        return r % 2 * ((r + 1) // 2) + (1 - r % 2) * ((NZ - r // 2) % NZ)

    upper = z // 9
    rank = 2 * (z + upper * (NZ - 2 * z)) - 1 + upper + (NZ - z) // NZ

    def greet_z(r, carry):
        greet((ranked(r) * NXY + xy, head))
        return carry

    lax.fori_loop(rank + 1, NZ, greet_z, 0)
    for rel in range(1, NXY):
        greet((xy_device(rel), head))
    for rel in range(1, 4):
        greet((ctx, (head + rel) % 4))

    loads["glat"].wait()
    own = glat[...].astype(F32).reshape(16, LAT + ROPE).astype(BF)
    keys[0, 0] = own[:, :HALF]
    keys[1, 0] = jnp.concatenate(
        [own[:, HALF:], jnp.zeros((16, 2 * HALF - LAT - ROPE), BF)], axis=1
    )

    def send_keys(there):
        pltpu.make_async_remote_copy(
            src_ref=keys.at[core, 0], dst_ref=keys.at[core, there - z],
            send_sem=key_send.at[there - z], recv_sem=key_recv.at[there - z],
            device_id=(there * NXY + xy, head), device_id_type=MESH,
        ).start()

    def to_lower(r, carry):
        there = ranked(r)

        @pl.when(there > z)
        def _():
            send_keys(there)

        @pl.when(there < z)
        def _():
            pl.semaphore_signal(
                here.at[z], inc=1, device_id=(there * NXY + xy, head), device_id_type=MESH
            )

        return carry

    def to_higher(r, carry):
        there = ranked(r)

        @pl.when(there > z)
        def _():
            pl.semaphore_wait(here.at[there], 1)
            send_keys(there)

        @pl.when(there < z)
        def _():
            took(keys.at[0, 1], key_recv.at[z - there])

        return carry

    def from_lower(r, carry):
        there = ranked(r)

        @pl.when(there < z)
        def _():
            took(keys.at[0, 1], key_recv.at[z - there])

        return carry

    pl.semaphore_wait(barrier, 10 + rank)
    lax.fori_loop(0, rank, to_lower, 0)
    loads["gq"].wait()
    queries[0] = gq[...].astype(F32).reshape(16, LOCAL * WIDE).astype(BF)
    for rel in range(NXY - 1, 0, -1):
        remote(queries.at[0], queries.at[back(rel)], 2, (xy_device(rel), head))

    loads["dq"].wait()
    rows = NXY * 16
    flat = dq[...].astype(F32).reshape(32, LOCAL * WIDE).astype(BF)
    row = iota((rows, 32), 0)
    pick = absolute(row // 16) * 4 + row % 4 == iota((rows, 32), 1)
    spread = dot(jnp.where(pick, 1.0, 0.0).astype(BF), flat)
    row = iota((rows, 1), 0)
    row_head = row // 4 % 4
    row_req = absolute(row // 16) // 2 % 2
    nope = jnp.concatenate(
        [
            jnp.where(row_head == h, spread[:, h * WIDE : h * WIDE + NOPE], 0.0)
            for h in range(LOCAL)
        ],
        axis=1,
    ).astype(BF)
    rope = jnp.zeros((rows, ROPE), F32)
    for h in range(LOCAL):
        rope = jnp.where(row_head == h, spread[:, h * WIDE + NOPE : (h + 1) * WIDE], rope)
    rope = rope.astype(BF)
    loads["wk"].wait()
    absorbed = dot_t(nope, wk[...]).astype(BF)

    loads["start"].wait()
    loads["cache"].wait()
    scores = []
    masks = []
    for r in range(2):
        got = dot(absorbed, cache[r, :LAT]) + dot(rope, cache[r, LAT:])
        position = ctx * 256 + iota((1, 256), 1)
        allowed = (position < start[r]) & (row_req == r)
        masks.append(allowed)
        scores.append(jnp.where(allowed, got * SCALE, LOW))
    got = dot_t(absorbed, own[:, :LAT]) + dot_t(rope, own[:, LAT:])
    allowed = iota((1, 16), 1) // 8 == row_req
    masks.append(allowed)
    scores.append(jnp.where(allowed, got * SCALE, LOW))
    peak = jnp.max(scores[0], axis=1, keepdims=True)
    for got in scores[1:]:
        peak = jnp.maximum(peak, jnp.max(got, axis=1, keepdims=True))
    total = jnp.zeros((rows, 1), F32)
    mixture = jnp.zeros((rows, LAT), F32)
    for k, (got, allowed) in enumerate(zip(scores, masks)):
        weights = jnp.where(allowed, jnp.exp(got - peak), 0.0)
        total = total + jnp.sum(weights, axis=1, keepdims=True)
        weights = weights.astype(BF)
        mixture = mixture + (
            dot_t(weights, cache[k, :LAT]) if k < 2 else dot(weights, own[:, :LAT])
        )
    loads["wv"].wait()
    wide = dot(mixture.astype(BF), wv[...])
    part = jnp.zeros((rows, NOPE), F32)
    for h in range(LOCAL):
        part = jnp.where(row_head == h, wide[:, h * 128 : (h + 1) * 128], part)
    stats = by_lane((rows, 128), dict(enumerate(split(peak, 3) + split(total, 2))))
    packed = jnp.concatenate([part, stats], axis=1).astype(BF).reshape(NXY, 16, 256)
    dsend[...] = packed
    drecv[0] = packed[0]
    for rel in range(NXY - 1, 0, -1):
        remote(dsend.at[rel], drecv.at[back(rel)], 3, (xy_device(rel), head))

    took(queries.at[1:NXY], recv_sem.at[2])
    all_q = queries[...].reshape(128, LOCAL * WIDE)
    for h in range(LOCAL):
        block = dot_t(all_q[:, h * WIDE : h * WIDE + NOPE], wk[:, h * 128 : (h + 1) * 128])
        big_q[h * 128 : (h + 1) * 128, :LAT] = block.astype(BF)
        big_q[h * 128 : (h + 1) * 128, LAT:] = jnp.concatenate(
            [
                all_q[:, h * WIDE + NOPE : (h + 1) * WIDE],
                jnp.zeros((128, 2 * HALF - LAT - ROPE), BF),
            ],
            axis=1,
        )

    lax.fori_loop(rank + 1, NZ, to_higher, 0)

    took(drecv.at[1:NXY], recv_sem.at[3])
    packed = drecv[...].astype(F32)
    peak, total, part = merge(packed[..., 128:], 0, packed[..., :128])
    stats = by_lane((16, 128), dict(enumerate(split(peak, 3) + split(total, 2))))
    zrecv[0] = jnp.concatenate([part, stats], axis=1).astype(BF)

    def send_z(j, carry):
        d = 8 + (j % 2 * 2 - 1) * ((j + 1) // 2)
        remote(zrecv.at[0], zrecv.at[NZ - d], 1, (z_device(d), head))
        return carry

    lax.fori_loop(0, NZ - 1, send_z, 0)

    lax.fori_loop(0, rank, from_lower, 0)
    remote(keys.at[core, 1:NZ], keys.at[core, 1:NZ], 0, (ctx, sibling))
    took(keys.at[0, 1:NZ], recv_sem.at[0])

    first = keys[0].reshape(256, HALF)
    second = keys[1].reshape(256, HALF)
    scores = dot_t(big_q[:, :HALF], first) + dot_t(big_q[:, HALF:], second)
    row = iota((LOCAL * 128, 1), 0)
    col = iota((1, 256), 1)
    query_at = (z * NXY + absolute(row // 16 % NXY)) * 8 + row % 8
    key_z = z - col // 16
    key_at = (key_z * NXY + xy) * 8 + col % 8
    allowed = (key_z >= 0) & (key_at <= query_at) & (row // 8 % 2 == col // 8 % 2)
    scores = jnp.where(allowed, scores * SCALE, LOW)
    peak = jnp.max(scores, axis=1, keepdims=True)
    weights = jnp.where(allowed, jnp.exp(scores - peak), 0.0)
    total = jnp.sum(weights, axis=1, keepdims=True)
    weights = weights.astype(BF)
    mixture = jnp.concatenate(
        [dot(weights, first), dot(weights, second[:, : LAT - HALF])], axis=1
    ).astype(BF)
    columns = {}
    for h in range(LOCAL):
        at = slice(h * 128, (h + 1) * 128)
        part = dot(mixture[at], wv[:, at]).astype(BF).reshape(NXY, 16, 128)
        gsend[:, :, at] = part
        grecv[0, :, at] = part[0]
        for k, column in enumerate(split(peak[at], 3) + split(total[at], 2)):
            columns[8 * h + k] = column
    stats = by_lane((128, 128), columns).astype(BF).reshape(NXY, 16, 128)
    gsend[:, :, LAT:] = stats
    grecv[0, :, LAT:] = stats[0]
    for rel in range(NXY - 1, 0, -1):
        remote(gsend.at[rel], grecv.at[back(rel)], 4, (xy_device(rel), head))

    took(zrecv.at[1:NZ], recv_sem.at[1])
    packed = zrecv[...].astype(F32)
    peak, total, part = merge(packed[..., 128:], 0, packed[..., :128])
    attention = (part / total).astype(BF)
    row = iota((64, 16), 0)
    pick = row // 16 * 4 + row % 4 == iota((64, 16), 1)
    spread = dot(jnp.where(pick, 1.0, 0.0).astype(BF), attention).astype(BF)
    lined = jnp.concatenate([spread[h * 16 : (h + 1) * 16] for h in range(LOCAL)], axis=1)
    loads["wo"].wait()
    hidden = dot(lined, wo[...])
    block = iota((16, 128), 0) // 4
    for j in range(4):
        tile = jnp.zeros((16, 128), F32)
        for c in range(4):
            at = j * 512 + c * 128
            tile = jnp.where(block == c, hidden[:, at : at + 128], tile)
        psend[j] = tile.astype(BF)
    precv[0] = psend[head]

    def send_plane(j, carry):
        k = 31 - j
        rel, turn = k // 4, k % 4
        there = (head + turn) % 4
        slot = back(rel) * 4 + (4 - turn) % 4
        remote(psend.at[there], precv.at[slot], 5, (xy_device(rel), there))
        return carry

    lax.fori_loop(0, 31, send_plane, 0)

    took(grecv.at[1:NXY], recv_sem.at[4])
    stats = grecv[:, :, LAT:].astype(F32)
    blocks = []
    for h in range(LOCAL):
        got = grecv[:, :, h * 128 : (h + 1) * 128].astype(F32)
        peak, total, part = merge(stats, 8 * h, got)
        blocks.append((part / total).astype(BF))
    hidden = dot(jnp.concatenate(blocks, axis=1), wo[...]).astype(BF)
    for j in range(4):
        hsend[j] = hidden[:, j * 512 : (j + 1) * 512]
    hrecv[0] = hsend[head]
    for turn in (2, 3, 1):
        there = (head + turn) % 4
        remote(hsend.at[there], hrecv.at[4 - turn], 6, (ctx, there))

    took(precv.at[1:32], recv_sem.at[5])
    summed = jnp.sum(precv[...].astype(F32).reshape(NXY, 4, 16, 128), axis=1)
    summed = summed.reshape(128, 128).astype(BF)
    row = iota((128, 128), 0)
    col = iota((128, 128), 1)
    pick = (row // 32 == col // 4 % 4) & (row % 32 == absolute(col // 16) * 4 + col % 4)
    placed = dot(jnp.where(pick, 1.0, 0.0).astype(BF), summed)
    decode_out[...] = (
        jnp.concatenate([placed[c * 32 : (c + 1) * 32] for c in range(4)], axis=1)
        .reshape(2, 2, 8, 512)
        .astype(BF)
    )
    took(hrecv.at[1:4], recv_sem.at[6])
    group_out[...] = (
        jnp.sum(hrecv[...].astype(F32), axis=0).reshape(2, 8, 512).astype(BF)
    )

    for phase, ref in (
        (0, keys.at[0, 1:NZ]), (2, queries.at[1:NXY]), (3, drecv.at[1:NXY]), (1, zrecv.at[1:NZ]),
        (4, grecv.at[1:NXY]), (5, precv.at[1:32]), (6, hrecv.at[1:4]),
    ):
        took(ref, send_sem.at[phase])

    def sent_keys(distance, carry):
        took(keys.at[0, 1], key_send.at[distance])
        return carry

    lax.fori_loop(1, NZ - z, sent_keys, 0)


def shards(
    cache_latent, group_latent, group_query, decode_query, group_start, w_key, w_value, w_out
):
    hbm = pl.BlockSpec(memory_space=pltpu.HBM)
    vmem = pl.BlockSpec(memory_space=pltpu.VMEM)
    return pl.pallas_call(
        kernel,
        out_shape=(
            jax.ShapeDtypeStruct((2, 8, 512), BF),
            jax.ShapeDtypeStruct((2, 2, 8, 512), BF),
        ),
        in_specs=[hbm] * 8,
        out_specs=(vmem, vmem),
        scratch_shapes=[
            pltpu.SMEM((2,), jnp.int32),
            pltpu.VMEM((2, 576, 256), BF),
            pltpu.VMEM((2, 8, 576), BF),
            pltpu.VMEM((2, 8, 768), BF),
            pltpu.VMEM((2, 2, 8, 768), BF),
            pltpu.VMEM((512, 512), BF),
            pltpu.VMEM((512, 512), BF),
            pltpu.VMEM((512, 2048), BF),
            pltpu.VMEM((2, NZ, 16, HALF), BF),
            pltpu.VMEM((NXY, 16, 768), BF),
            pltpu.VMEM((512, 2 * HALF), BF),
            pltpu.VMEM((NXY, 16, 256), BF),
            pltpu.VMEM((NXY, 16, 256), BF),
            pltpu.VMEM((NZ, 16, 256), BF),
            pltpu.VMEM((4, 16, 128), BF),
            pltpu.VMEM((32, 16, 128), BF),
            pltpu.VMEM((NXY, 16, 640), BF),
            pltpu.VMEM((NXY, 16, 640), BF),
            pltpu.VMEM((4, 16, 512), BF),
            pltpu.VMEM((4, 16, 512), BF),
            pltpu.SemaphoreType.DMA((8,)),
            pltpu.SemaphoreType.DMA((7,)),
            pltpu.SemaphoreType.DMA((7,)),
            pltpu.SemaphoreType.DMA((NZ,)),
            pltpu.SemaphoreType.DMA((NZ,)),
            pltpu.SemaphoreType.REGULAR((NZ,)),
        ],
        compiler_params=pltpu.CompilerParams(
            collective_id=0, has_side_effects=True, vmem_limit_bytes=32 << 20
        ),
        name="latent_attention",
    )(
        *(
            pltpu.with_memory_space_constraint(array, pltpu.HBM)
            for array in (
                group_start, cache_latent.transpose(0, 2, 1), group_latent, group_query,
                decode_query, w_key, w_value, w_out,
            )
        )
    )


def solution(mesh):
    in_specs = (
        P(None, "ctx", None),
        P(None, "ctx", None),
        P(None, "ctx", "head"),
        P(None, None, None, "head"),
        P(),
        P(None, "head"),
        P(None, "head"),
        P("head", None),
    )
    out_specs = (P(None, "ctx", "head"), P(None, None, None, "head"))
    return jax.shard_map(shards, mesh=mesh, in_specs=in_specs, out_specs=out_specs, check_vma=False)
```

```python
import jax
import jax.numpy as jnp
from jax import lax
from jax.experimental import pallas as pl
from jax.experimental.pallas import tpu as pltpu
from jax.sharding import PartitionSpec as P

MESH = pl.DeviceIdType.MESH
BF = jnp.bfloat16
F32 = jnp.float32
LAT = 512
ROPE = 64
NOPE = 128
WIDE = NOPE + ROPE
PADDED = 640
SPLIT = 256
LOCAL = 4
NZ = 16
NXY = 8
SCALE = 1.0 / WIDE**0.5
LOW = -1e30


def dot(a, b):
    return lax.dot_general(a, b, (((1,), (0,)), ((), ())), preferred_element_type=F32)


def dot_t(a, b):
    return lax.dot_general(a, b, (((1,), (1,)), ((), ())), preferred_element_type=F32)


def iota(shape, axis):
    return lax.broadcasted_iota(jnp.int32, shape, axis)


def split(value, pieces):
    out = []
    for _ in range(pieces):
        head = value.astype(BF).astype(F32)
        out.append(head)
        value = value - head
    return out


def by_lane(shape, columns):
    lane = iota(shape, 1)
    tile = jnp.zeros(shape, F32)
    for at, column in columns.items():
        tile = jnp.where(lane == at, column, tile)
    return tile


def merge(stats, at, blocks):
    peak = stats[..., at : at + 1] + stats[..., at + 1 : at + 2] + stats[..., at + 2 : at + 3]
    total = stats[..., at + 3 : at + 4] + stats[..., at + 4 : at + 5]
    top = jnp.max(peak, axis=0, keepdims=True)
    factor = jnp.exp(peak - top)
    return top[0], jnp.sum(factor * total, axis=0), jnp.sum(factor * blocks, axis=0)


def kernel(
    start_hbm, cache_hbm, glat_hbm, gq_hbm, dq_hbm, wk_hbm, wv_hbm, wo_hbm,
    group_out, decode_out,
    start, cache, glat, gq, dq, wk, wv, wo,
    keys_a, keys_b, queries, big_q, dsend, drecv, zrecv, zstat, psend, precv, gsend, grecv, hsend, hrecv,
    local_sem, send_sem, recv_sem, key_send, key_recv, here,
):
    ctx = lax.axis_index("ctx")
    head = lax.axis_index("head")
    z = ctx // NXY
    xy = ctx % NXY
    yl = xy // 4
    x = xy % 4
    core = head % 2
    sibling = head // 2 * 2 + (1 - core)

    def xy_device(rel):
        dy, dx = rel // 4, rel % 4
        return z * NXY + (yl + dy) % 2 * 4 + (x + dx) % 4

    def back(rel):
        return rel // 4 * 4 + (4 - rel % 4) % 4

    def z_device(d):
        return (z + d) % NZ * NXY + xy

    def absolute(rel):
        return (yl + rel // 4) % 2 * 4 + (x + rel % 4) % 4

    def remote(src, dst, phase, device):
        pltpu.make_async_remote_copy(
            src_ref=src, dst_ref=dst, send_sem=send_sem.at[phase], recv_sem=recv_sem.at[phase],
            device_id=device, device_id_type=MESH,
        ).start()

    def took(ref, sem):
        pltpu.make_async_copy(ref, ref, sem).wait()

    loads = {}
    for at, (name, src, dst) in enumerate((
        ("glat", glat_hbm, glat), ("gq", gq_hbm, gq), ("dq", dq_hbm, dq), ("wk", wk_hbm, wk),
        ("start", start_hbm, start), ("cache", cache_hbm, cache), ("wv", wv_hbm, wv),
        ("wo", wo_hbm, wo),
    )):
        loads[name] = pltpu.make_async_copy(src, dst, local_sem.at[at])
        if name != "wo":
            loads[name].start()
    keys_a[...] = jnp.zeros_like(keys_a)
    keys_b[...] = jnp.zeros_like(keys_b)
    barrier = pltpu.get_barrier_semaphore()

    def greet(device):
        pl.semaphore_signal(barrier, inc=1, device_id=device, device_id_type=MESH)

    def ranked(r):
        return r

    rank = z

    def greet_z(r, carry):
        greet((ranked(r) * NXY + xy, head))
        return carry

    lax.fori_loop(rank + 1, NZ, greet_z, 0)
    for rel in range(1, NXY):
        greet((xy_device(rel), head))
    for rel in range(1, 4):
        greet((ctx, (head + rel) % 4))

    loads["glat"].wait()
    own = glat[...].astype(F32).reshape(16, LAT + ROPE).astype(BF)
    keys_a[0] = own[:, :SPLIT]
    keys_b[0] = jnp.concatenate([own[:, SPLIT:], jnp.zeros((16, PADDED - LAT - ROPE), BF)], axis=1)

    def on_core(action):
        for at, keys in enumerate((keys_a, keys_b)):

            @pl.when(core == at)
            def _(keys=keys):
                action(keys)

    def send_keys(there):
        on_core(
            lambda keys: pltpu.make_async_remote_copy(
                src_ref=keys.at[0], dst_ref=keys.at[there - z],
                send_sem=key_send.at[there - z], recv_sem=key_recv.at[there - z],
                device_id=(there * NXY + xy, head), device_id_type=MESH,
            ).start()
        )

    def to_lower(r, carry):
        there = ranked(r)

        @pl.when(there > z)
        def _():
            send_keys(there)

        @pl.when(there < z)
        def _():
            pl.semaphore_signal(
                here.at[z], inc=1, device_id=(there * NXY + xy, head), device_id_type=MESH
            )

        return carry

    def send_z(there):
        slot = (z - there + NZ) % NZ
        remote(zrecv.at[0], zrecv.at[slot], 1, (there * NXY + xy, head))
        remote(zstat.at[0], zstat.at[slot], 7, (there * NXY + xy, head))

    def part_to_lower(r, carry):
        send_z(ranked(r))
        return carry

    def to_higher(j, carry):
        there = (z + (j + 1) // 2 * (2 * (j % 2) - 1) + NZ) % NZ

        @pl.when(there > rank)
        def _():
            @pl.when(there > z + 3)
            def _():
                pl.semaphore_wait(here.at[there], 1)
                send_keys(there)

            send_z(there)

        return carry

    def keys_to_next(there, carry):
        pl.semaphore_wait(here.at[there], 1)
        send_keys(there)
        return carry

    def from_lower(r, carry):
        there = ranked(r)

        @pl.when(there < z)
        def _():
            on_core(lambda keys: took(keys.at[1], key_recv.at[z - there]))

        return carry

    loads["dq"].wait()
    rows = NXY * 16
    flat = dq[...].astype(F32).reshape(32, LOCAL * WIDE).astype(BF)
    row = iota((rows, 32), 0)
    pick = absolute(row // 16) * 4 + row % 4 == iota((rows, 32), 1)
    spread = dot(jnp.where(pick, 1.0, 0.0).astype(BF), flat)
    row = iota((rows, 1), 0)
    row_head = row // 4 % 4
    row_req = absolute(row // 16) // 2 % 2
    nope = jnp.concatenate(
        [
            jnp.where(row_head == h, spread[:, h * WIDE : h * WIDE + NOPE], 0.0)
            for h in range(LOCAL)
        ],
        axis=1,
    ).astype(BF)
    rope = jnp.zeros((rows, ROPE), F32)
    for h in range(LOCAL):
        rope = jnp.where(row_head == h, spread[:, h * WIDE + NOPE : (h + 1) * WIDE], rope)
    rope = rope.astype(BF)
    loads["wk"].wait()
    absorbed = dot_t(nope, wk[...]).astype(BF)

    loads["start"].wait()
    loads["cache"].wait()
    scores = []
    masks = []
    for r in range(2):
        got = dot(absorbed, cache[r, :LAT]) + dot(rope, cache[r, LAT:])
        position = ctx * 256 + iota((1, 256), 1)
        allowed = (position < start[r]) & (row_req == r)
        masks.append(allowed)
        scores.append(jnp.where(allowed, got * SCALE, LOW))
    got = dot_t(absorbed, own[:, :LAT]) + dot_t(rope, own[:, LAT:])
    allowed = iota((1, 16), 1) // 8 == row_req
    masks.append(allowed)
    scores.append(jnp.where(allowed, got * SCALE, LOW))
    peak = jnp.max(scores[0], axis=1, keepdims=True)
    for got in scores[1:]:
        peak = jnp.maximum(peak, jnp.max(got, axis=1, keepdims=True))
    total = jnp.zeros((rows, 1), F32)
    mixture = jnp.zeros((rows, LAT), F32)
    for k, (got, allowed) in enumerate(zip(scores, masks)):
        weights = jnp.where(allowed, jnp.exp(got - peak), 0.0)
        total = total + jnp.sum(weights, axis=1, keepdims=True)
        weights = weights.astype(BF)
        mixture = mixture + (
            dot_t(weights, cache[k, :LAT]) if k < 2 else dot(weights, own[:, :LAT])
        )
    loads["wv"].wait()
    wide = dot(mixture.astype(BF), wv[...])
    part = jnp.zeros((rows, NOPE), F32)
    for h in range(LOCAL):
        part = jnp.where(row_head == h, wide[:, h * 128 : (h + 1) * 128], part)
    stats = by_lane((rows, 128), dict(enumerate(split(peak, 3) + split(total, 2))))
    packed = jnp.concatenate([part, stats], axis=1).astype(BF).reshape(NXY, 16, 256)
    dsend[...] = packed
    drecv[0] = packed[0]
    pl.semaphore_wait(barrier, 10 + rank)
    for rel in (6, 2, 5, 7, 4, 1, 3):
        remote(dsend.at[rel], drecv.at[back(rel)], 3, (xy_device(rel), head))

    lax.fori_loop(0, rank, to_lower, 0)
    loads["gq"].wait()
    queries[0] = gq[...].astype(F32).reshape(16, LOCAL * WIDE).astype(BF)
    for rel in (6, 2, 5, 7, 4, 1, 3):
        remote(queries.at[0], queries.at[back(rel)], 2, (xy_device(rel), head))

    loads["wo"].start()

    lax.fori_loop(z + 1, jnp.minimum(z + 4, NZ), keys_to_next, 0)

    took(drecv.at[1:NXY], recv_sem.at[3])
    packed = drecv[...].astype(F32)
    peak, total, part = merge(packed[..., 128:], 0, packed[..., :128])
    zrecv[0] = part.astype(BF)
    lane, row = iota((16, 128), 1), iota((16, 128), 0)
    zstat[0] = jnp.sum(
        jnp.where(lane == row, peak, jnp.where(lane == row + 16, total, 0.0)),
        axis=0, keepdims=True,
    )

    lax.fori_loop(0, rank, part_to_lower, 0)
    lax.fori_loop(1, NZ, to_higher, 0)

    took(queries.at[1:NXY], recv_sem.at[2])
    all_q = queries[...].reshape(128, LOCAL * WIDE)
    for h in range(LOCAL):
        block = dot_t(all_q[:, h * WIDE : h * WIDE + NOPE], wk[:, h * 128 : (h + 1) * 128])
        big_q[h * 128 : (h + 1) * 128, :LAT] = block.astype(BF)
        big_q[h * 128 : (h + 1) * 128, LAT:] = jnp.concatenate(
            [
                all_q[:, h * WIDE + NOPE : (h + 1) * WIDE],
                jnp.zeros((128, PADDED - LAT - ROPE), BF),
            ],
            axis=1,
        )

    lax.fori_loop(0, rank, from_lower, 0)
    on_core(lambda keys: remote(keys.at[1:NZ], keys.at[1:NZ], 0, (ctx, sibling)))
    for at, keys in enumerate((keys_b, keys_a)):

        @pl.when(core == at)
        def _(keys=keys):
            took(keys.at[1:NZ], recv_sem.at[0])


    first = keys_a[...].reshape(256, SPLIT)
    second = keys_b[...].reshape(256, PADDED - SPLIT)
    scores = dot_t(big_q[:, :SPLIT], first) + dot_t(big_q[:, SPLIT:], second)
    row = iota((LOCAL * 128, 1), 0)
    col = iota((1, 256), 1)
    query_at = (z * NXY + absolute(row // 16 % NXY)) * 8 + row % 8
    key_z = z - col // 16
    key_at = (key_z * NXY + xy) * 8 + col % 8
    allowed = (key_z >= 0) & (key_at <= query_at) & (row // 8 % 2 == col // 8 % 2)
    scores = jnp.where(allowed, scores * SCALE, LOW)
    peak = jnp.max(scores, axis=1, keepdims=True)
    weights = jnp.where(allowed, jnp.exp(scores - peak), 0.0)
    total = jnp.sum(weights, axis=1, keepdims=True)
    weights = weights.astype(BF)
    mixture = jnp.concatenate(
        [dot(weights, first), dot(weights, second[:, : LAT - SPLIT])], axis=1
    ).astype(BF)
    columns = {}
    for h in range(LOCAL):
        at = slice(h * 128, (h + 1) * 128)
        part = dot(mixture[at], wv[:, at]).astype(BF).reshape(NXY, 16, 128)
        gsend[:, :, at] = part
        grecv[0, :, at] = part[0]
        for k, column in enumerate(split(peak[at], 3) + split(total[at], 2)):
            columns[8 * h + k] = column
    stats = by_lane((128, 128), columns).astype(BF).reshape(NXY, 16, 128)
    gsend[:, :, LAT:] = stats
    grecv[0, :, LAT:] = stats[0]
    for rel in (6, 2, 5, 7, 4, 1, 3):
        remote(gsend.at[rel], grecv.at[back(rel)], 4, (xy_device(rel), head))

    took(zrecv.at[1:NZ], recv_sem.at[1])
    took(zstat.at[1:NZ], recv_sem.at[7])
    lane, row = iota((NZ, 16, 128), 2), iota((NZ, 16, 128), 1)
    peak = jnp.sum(jnp.where(lane == row, zstat[...], 0.0), axis=2, keepdims=True)
    total = jnp.sum(jnp.where(lane == row + 16, zstat[...], 0.0), axis=2, keepdims=True)
    factor = jnp.exp(peak - jnp.max(peak, axis=0, keepdims=True))
    part = jnp.sum(factor * zrecv[...].astype(F32), axis=0)
    attention = (part / jnp.sum(factor * total, axis=0)).astype(BF)
    row = iota((64, 16), 0)
    pick = row // 16 * 4 + row % 4 == iota((64, 16), 1)
    spread = dot(jnp.where(pick, 1.0, 0.0).astype(BF), attention).astype(BF)
    lined = jnp.concatenate([spread[h * 16 : (h + 1) * 16] for h in range(LOCAL)], axis=1)
    loads["wo"].wait()
    hidden = dot(lined, wo[...])
    block = iota((16, 128), 0) // 4
    for j in range(4):
        tile = jnp.zeros((16, 128), F32)
        for c in range(4):
            at = j * 512 + c * 128
            tile = jnp.where(block == c, hidden[:, at : at + 128], tile)
        psend[j] = tile.astype(BF)
    precv[0] = psend[head]

    for turn in (2, 1, 3, 0):
        there = (head + turn) % 4

        def send_plane(j, carry, turn=turn, there=there):
            rel = (j + 6) % NXY if turn else NXY - 1 - j
            slot = back(rel) * 4 + (4 - turn) % 4
            remote(psend.at[there], precv.at[slot], 5, (xy_device(rel), there))
            return carry

        lax.fori_loop(0, NXY if turn else NXY - 1, send_plane, 0)

    took(grecv.at[1:NXY], recv_sem.at[4])
    stats = grecv[:, :, LAT:].astype(F32)
    blocks = []
    for h in range(LOCAL):
        got = grecv[:, :, h * 128 : (h + 1) * 128].astype(F32)
        peak, total, part = merge(stats, 8 * h, got)
        blocks.append((part / total).astype(BF))
    hidden = dot(jnp.concatenate(blocks, axis=1), wo[...]).astype(BF)
    for j in range(4):
        hsend[j] = hidden[:, j * 512 : (j + 1) * 512]
    hrecv[0] = hsend[head]
    for turn in (2, 3, 1):
        there = (head + turn) % 4
        remote(hsend.at[there], hrecv.at[4 - turn], 6, (ctx, there))

    took(precv.at[1:32], recv_sem.at[5])
    summed = jnp.sum(precv[...].astype(F32).reshape(NXY, 4, 16, 128), axis=1)
    summed = summed.reshape(128, 128).astype(BF)
    row = iota((128, 128), 0)
    col = iota((128, 128), 1)
    pick = (row // 32 == col // 4 % 4) & (row % 32 == absolute(col // 16) * 4 + col % 4)
    placed = dot(jnp.where(pick, 1.0, 0.0).astype(BF), summed)
    decode_out[...] = (
        jnp.concatenate([placed[c * 32 : (c + 1) * 32] for c in range(4)], axis=1)
        .reshape(2, 2, 8, 512)
        .astype(BF)
    )
    took(hrecv.at[1:4], recv_sem.at[6])
    group_out[...] = (
        jnp.sum(hrecv[...].astype(F32), axis=0).reshape(2, 8, 512).astype(BF)
    )

    for phase, ref in (
        (2, queries.at[1:NXY]), (3, drecv.at[1:NXY]), (1, zrecv.at[1:NZ]),
        (7, zstat.at[1:NZ]),
        (4, grecv.at[1:NXY]), (5, precv.at[1:32]), (6, hrecv.at[1:4]),
    ):
        took(ref, send_sem.at[phase])

    on_core(lambda keys: took(keys.at[1:NZ], send_sem.at[0]))

    def sent_keys(distance, carry):
        on_core(lambda keys: took(keys.at[1], key_send.at[distance]))
        return carry

    lax.fori_loop(1, NZ - z, sent_keys, 0)


def shards(
    cache_latent, group_latent, group_query, decode_query, group_start, w_key, w_value, w_out
):
    hbm = pl.BlockSpec(memory_space=pltpu.HBM)
    vmem = pl.BlockSpec(memory_space=pltpu.VMEM)
    return pl.pallas_call(
        kernel,
        out_shape=(
            jax.ShapeDtypeStruct((2, 8, 512), BF),
            jax.ShapeDtypeStruct((2, 2, 8, 512), BF),
        ),
        in_specs=[hbm] * 8,
        out_specs=(vmem, vmem),
        scratch_shapes=[
            pltpu.SMEM((2,), jnp.int32),
            pltpu.VMEM((2, 576, 256), BF),
            pltpu.VMEM((2, 8, 576), BF),
            pltpu.VMEM((2, 8, 768), BF),
            pltpu.VMEM((2, 2, 8, 768), BF),
            pltpu.VMEM((512, 512), BF),
            pltpu.VMEM((512, 512), BF),
            pltpu.VMEM((512, 2048), BF),
            pltpu.VMEM((NZ, 16, SPLIT), BF),
            pltpu.VMEM((NZ, 16, PADDED - SPLIT), BF),
            pltpu.VMEM((NXY, 16, 768), BF),
            pltpu.VMEM((512, PADDED), BF),
            pltpu.VMEM((NXY, 16, 256), BF),
            pltpu.VMEM((NXY, 16, 256), BF),
            pltpu.VMEM((NZ, 16, 128), BF),
            pltpu.VMEM((NZ, 1, 128), F32),
            pltpu.VMEM((4, 16, 128), BF),
            pltpu.VMEM((32, 16, 128), BF),
            pltpu.VMEM((NXY, 16, 640), BF),
            pltpu.VMEM((NXY, 16, 640), BF),
            pltpu.VMEM((4, 16, 512), BF),
            pltpu.VMEM((4, 16, 512), BF),
            pltpu.SemaphoreType.DMA((8,)),
            pltpu.SemaphoreType.DMA((8,)),
            pltpu.SemaphoreType.DMA((8,)),
            pltpu.SemaphoreType.DMA((NZ,)),
            pltpu.SemaphoreType.DMA((NZ,)),
            pltpu.SemaphoreType.REGULAR((NZ,)),
        ],
        compiler_params=pltpu.CompilerParams(
            collective_id=0, has_side_effects=True, vmem_limit_bytes=32 << 20
        ),
        name="latent_attention",
    )(
        *(
            pltpu.with_memory_space_constraint(array, pltpu.HBM)
            for array in (
                group_start, cache_latent.transpose(0, 2, 1), group_latent, group_query,
                decode_query, w_key, w_value, w_out,
            )
        )
    )


def solution(mesh):
    in_specs = (
        P(None, "ctx", None),
        P(None, "ctx", None),
        P(None, "ctx", "head"),
        P(None, None, None, "head"),
        P(),
        P(None, "head"),
        P(None, "head"),
        P("head", None),
    )
    out_specs = (P(None, "ctx", "head"), P(None, None, None, "head"))
    return jax.shard_map(shards, mesh=mesh, in_specs=in_specs, out_specs=out_specs, check_vma=False)
```

```python
import jax
import jax.numpy as jnp
from jax import lax
from jax.experimental import pallas as pl
from jax.experimental.pallas import tpu as pltpu
from jax.sharding import PartitionSpec as P

MESH = pl.DeviceIdType.MESH
BF = jnp.bfloat16
F32 = jnp.float32
LAT = 512
ROPE = 64
NOPE = 128
WIDE = NOPE + ROPE
PADDED = 640
SPLIT = 256
LOCAL = 4
NZ = 16
NXY = 8
SCALE = 1.0 / WIDE**0.5
LOW = -1e30


def dot(a, b):
    return lax.dot_general(a, b, (((1,), (0,)), ((), ())), preferred_element_type=F32)


def dot_t(a, b):
    return lax.dot_general(a, b, (((1,), (1,)), ((), ())), preferred_element_type=F32)


def iota(shape, axis):
    return lax.broadcasted_iota(jnp.int32, shape, axis)


def split(value, pieces):
    out = []
    for _ in range(pieces):
        head = value.astype(BF).astype(F32)
        out.append(head)
        value = value - head
    return out


def by_lane(shape, columns):
    lane = iota(shape, 1)
    tile = jnp.zeros(shape, F32)
    for at, column in columns.items():
        tile = jnp.where(lane == at, column, tile)
    return tile


def merge(stats, at, blocks):
    peak = stats[..., at : at + 1] + stats[..., at + 1 : at + 2] + stats[..., at + 2 : at + 3]
    total = stats[..., at + 3 : at + 4] + stats[..., at + 4 : at + 5]
    top = jnp.max(peak, axis=0, keepdims=True)
    factor = jnp.exp(peak - top)
    return top[0], jnp.sum(factor * total, axis=0), jnp.sum(factor * blocks, axis=0)


def kernel(
    start_hbm, cache_hbm, glat_hbm, gq_hbm, dq_hbm, wk_hbm, wv_hbm, wo_hbm,
    group_out, decode_out,
    start, cache, glat, gq, dq, wk, wv, wo,
    keys_a, keys_b, queries, big_q, dsend, drecv, zrecv, zstat, final, psend, precv,
    gsend, grecv, hsend, hrecv,
    local_sem, send_sem, recv_sem, key_send, key_recv, here,
):
    ctx = lax.axis_index("ctx")
    head = lax.axis_index("head")
    z = ctx // NXY
    xy = ctx % NXY
    yl = xy // 4
    x = xy % 4
    core = head % 2
    sibling = head // 2 * 2 + (1 - core)

    def xy_device(rel):
        dy, dx = rel // 4, rel % 4
        return z * NXY + (yl + dy) % 2 * 4 + (x + dx) % 4

    def back(rel):
        return rel // 4 * 4 + (4 - rel % 4) % 4

    def z_device(d):
        return (z + d) % NZ * NXY + xy

    def absolute(rel):
        return (yl + rel // 4) % 2 * 4 + (x + rel % 4) % 4

    def remote(src, dst, phase, device):
        pltpu.make_async_remote_copy(
            src_ref=src, dst_ref=dst, send_sem=send_sem.at[phase], recv_sem=recv_sem.at[phase],
            device_id=device, device_id_type=MESH,
        ).start()

    def took(ref, sem):
        pltpu.make_async_copy(ref, ref, sem).wait()

    loads = {}
    for at, (name, src, dst) in enumerate((
        ("glat", glat_hbm, glat), ("gq", gq_hbm, gq), ("dq", dq_hbm, dq), ("wk", wk_hbm, wk),
        ("start", start_hbm, start), ("cache", cache_hbm, cache), ("wv", wv_hbm, wv),
        ("wo", wo_hbm, wo),
    )):
        loads[name] = pltpu.make_async_copy(src, dst, local_sem.at[at])
        if name != "wo":
            loads[name].start()
    keys_a[...] = jnp.zeros_like(keys_a)
    keys_b[...] = jnp.zeros_like(keys_b)
    barrier = pltpu.get_barrier_semaphore()

    def greet(device):
        pl.semaphore_signal(barrier, inc=1, device_id=device, device_id_type=MESH)

    def ranked(r):
        return r

    rank = z

    def greet_z(r, carry):
        greet((ranked(r) * NXY + xy, head))
        return carry

    lax.fori_loop(rank + 1, NZ, greet_z, 0)
    for rel in range(1, NXY):
        greet((xy_device(rel), head))
    for rel in range(1, 4):
        greet((ctx, (head + rel) % 4))

    loads["glat"].wait()
    own = glat[...].astype(F32).reshape(16, LAT + ROPE).astype(BF)
    keys_a[0] = own[:, :SPLIT]
    keys_b[0] = jnp.concatenate([own[:, SPLIT:], jnp.zeros((16, PADDED - LAT - ROPE), BF)], axis=1)

    def on_core(action):
        for at, keys in enumerate((keys_a, keys_b)):

            @pl.when(core == at)
            def _(keys=keys):
                action(keys)

    def send_keys(there):
        on_core(
            lambda keys: pltpu.make_async_remote_copy(
                src_ref=keys.at[0], dst_ref=keys.at[there - z],
                send_sem=key_send.at[there - z], recv_sem=key_recv.at[there - z],
                device_id=(there * NXY + xy, head), device_id_type=MESH,
            ).start()
        )

    def to_lower(r, carry):
        there = ranked(r)

        @pl.when(there > z)
        def _():
            send_keys(there)

        @pl.when(there < z)
        def _():
            pl.semaphore_signal(
                here.at[z], inc=1, device_id=(there * NXY + xy, head), device_id_type=MESH
            )

        return carry

    def send_z(there):
        slot = (z - there + NZ) % NZ
        remote(zrecv.at[0], zrecv.at[slot], 1, (there * NXY + xy, head))
        remote(zstat.at[0], zstat.at[slot], 7, (there * NXY + xy, head))

    def part_to_lower(r, carry):
        send_z(r)
        return carry

    def ahead(j):
        return (z + (j + 1) // 2 * (2 * (j % 2) - 1) + NZ) % NZ

    def keys_to_higher(j, carry):
        there = ahead(j)

        @pl.when(there > z + 3)
        def _():
            pl.semaphore_wait(here.at[there], 1)
            send_keys(there)

        return carry

    def part_to_higher(j, carry):
        there = ahead(j)

        @pl.when((there > z) & (there < 8))
        def _():
            send_z(there)

        return carry

    def keys_to_next(there, carry):
        pl.semaphore_wait(here.at[there], 1)
        send_keys(there)
        return carry

    def from_lower(r, carry):
        there = ranked(r)

        @pl.when(there < z)
        def _():
            on_core(lambda keys: took(keys.at[1], key_recv.at[z - there]))

        return carry

    loads["dq"].wait()
    rows = NXY * 16
    flat = dq[...].astype(F32).reshape(32, LOCAL * WIDE).astype(BF)
    row = iota((rows, 32), 0)
    pick = absolute(row // 16) * 4 + row % 4 == iota((rows, 32), 1)
    spread = dot(jnp.where(pick, 1.0, 0.0).astype(BF), flat)
    row = iota((rows, 1), 0)
    row_head = row // 4 % 4
    row_req = absolute(row // 16) // 2 % 2
    nope = jnp.concatenate(
        [
            jnp.where(row_head == h, spread[:, h * WIDE : h * WIDE + NOPE], 0.0)
            for h in range(LOCAL)
        ],
        axis=1,
    ).astype(BF)
    rope = jnp.zeros((rows, ROPE), F32)
    for h in range(LOCAL):
        rope = jnp.where(row_head == h, spread[:, h * WIDE + NOPE : (h + 1) * WIDE], rope)
    rope = rope.astype(BF)
    loads["wk"].wait()
    absorbed = dot_t(nope, wk[...]).astype(BF)

    loads["start"].wait()
    loads["cache"].wait()
    scores = []
    masks = []
    for r in range(2):
        got = dot(absorbed, cache[r, :LAT]) + dot(rope, cache[r, LAT:])
        position = ctx * 256 + iota((1, 256), 1)
        allowed = (position < start[r]) & (row_req == r)
        masks.append(allowed)
        scores.append(jnp.where(allowed, got * SCALE, LOW))
    got = dot_t(absorbed, own[:, :LAT]) + dot_t(rope, own[:, LAT:])
    allowed = iota((1, 16), 1) // 8 == row_req
    masks.append(allowed)
    scores.append(jnp.where(allowed, got * SCALE, LOW))
    peak = jnp.max(scores[0], axis=1, keepdims=True)
    for got in scores[1:]:
        peak = jnp.maximum(peak, jnp.max(got, axis=1, keepdims=True))
    total = jnp.zeros((rows, 1), F32)
    mixture = jnp.zeros((rows, LAT), F32)
    for k, (got, allowed) in enumerate(zip(scores, masks)):
        weights = jnp.where(allowed, jnp.exp(got - peak), 0.0)
        total = total + jnp.sum(weights, axis=1, keepdims=True)
        weights = weights.astype(BF)
        mixture = mixture + (
            dot_t(weights, cache[k, :LAT]) if k < 2 else dot(weights, own[:, :LAT])
        )
    loads["wv"].wait()
    wide = dot(mixture.astype(BF), wv[...])
    part = jnp.zeros((rows, NOPE), F32)
    for h in range(LOCAL):
        part = jnp.where(row_head == h, wide[:, h * 128 : (h + 1) * 128], part)
    stats = by_lane((rows, 128), dict(enumerate(split(peak, 3) + split(total, 2))))
    packed = jnp.concatenate([part, stats], axis=1).astype(BF).reshape(NXY, 16, 256)
    dsend[...] = packed
    drecv[0] = packed[0]
    pl.semaphore_wait(barrier, 10 + rank)
    for rel in (6, 2, 5, 7, 4, 1, 3):
        remote(dsend.at[rel], drecv.at[back(rel)], 3, (xy_device(rel), head))

    lax.fori_loop(0, rank, to_lower, 0)
    loads["gq"].wait()
    queries[0] = gq[...].astype(F32).reshape(16, LOCAL * WIDE).astype(BF)
    for rel in (6, 2, 5, 7, 4, 1, 3):
        remote(queries.at[0], queries.at[back(rel)], 2, (xy_device(rel), head))

    loads["wo"].start()

    lax.fori_loop(z + 1, jnp.minimum(z + 4, NZ), keys_to_next, 0)

    took(drecv.at[1:NXY], recv_sem.at[3])
    packed = drecv[...].astype(F32)
    peak, total, part = merge(packed[..., 128:], 0, packed[..., :128])
    zrecv[0] = part.astype(BF)
    lane, row = iota((16, 128), 1), iota((16, 128), 0)
    zstat[0] = jnp.sum(
        jnp.where(lane == row, peak, jnp.where(lane == row + 16, total, 0.0)),
        axis=0, keepdims=True,
    )

    lax.fori_loop(0, jnp.minimum(z, 8), part_to_lower, 0)
    lax.fori_loop(1, NZ, keys_to_higher, 0)
    lax.fori_loop(1, NZ, part_to_higher, 0)

    took(queries.at[1:NXY], recv_sem.at[2])
    all_q = queries[...].reshape(128, LOCAL * WIDE)
    for h in range(LOCAL):
        block = dot_t(all_q[:, h * WIDE : h * WIDE + NOPE], wk[:, h * 128 : (h + 1) * 128])
        big_q[h * 128 : (h + 1) * 128, :LAT] = block.astype(BF)
        big_q[h * 128 : (h + 1) * 128, LAT:] = jnp.concatenate(
            [
                all_q[:, h * WIDE + NOPE : (h + 1) * WIDE],
                jnp.zeros((128, PADDED - LAT - ROPE), BF),
            ],
            axis=1,
        )

    lax.fori_loop(0, rank, from_lower, 0)
    on_core(lambda keys: remote(keys.at[1:NZ], keys.at[1:NZ], 0, (ctx, sibling)))
    for at, keys in enumerate((keys_b, keys_a)):

        @pl.when(core == at)
        def _(keys=keys):
            took(keys.at[1:NZ], recv_sem.at[0])


    first = keys_a[...].reshape(256, SPLIT)
    second = keys_b[...].reshape(256, PADDED - SPLIT)
    scores = dot_t(big_q[:, :SPLIT], first) + dot_t(big_q[:, SPLIT:], second)
    row = iota((LOCAL * 128, 1), 0)
    col = iota((1, 256), 1)
    query_at = (z * NXY + absolute(row // 16 % NXY)) * 8 + row % 8
    key_z = z - col // 16
    key_at = (key_z * NXY + xy) * 8 + col % 8
    allowed = (key_z >= 0) & (key_at <= query_at) & (row // 8 % 2 == col // 8 % 2)
    scores = jnp.where(allowed, scores * SCALE, LOW)
    peak = jnp.max(scores, axis=1, keepdims=True)
    weights = jnp.where(allowed, jnp.exp(scores - peak), 0.0)
    total = jnp.sum(weights, axis=1, keepdims=True)
    weights = weights.astype(BF)
    mixture = jnp.concatenate(
        [dot(weights, first), dot(weights, second[:, : LAT - SPLIT])], axis=1
    ).astype(BF)
    columns = {}
    for h in range(LOCAL):
        at = slice(h * 128, (h + 1) * 128)
        part = dot(mixture[at], wv[:, at]).astype(BF).reshape(NXY, 16, 128)
        gsend[:, :, at] = part
        grecv[0, :, at] = part[0]
        for k, column in enumerate(split(peak[at], 3) + split(total[at], 2)):
            columns[8 * h + k] = column
    stats = by_lane((128, 128), columns).astype(BF).reshape(NXY, 16, 128)
    gsend[:, :, LAT:] = stats
    grecv[0, :, LAT:] = stats[0]
    for rel in (6, 2, 5, 7, 4, 1, 3):
        remote(gsend.at[rel], grecv.at[back(rel)], 4, (xy_device(rel), head))

    @pl.when(z < 8)
    def _():
        took(zrecv.at[1:NZ], recv_sem.at[1])
        took(zstat.at[1:NZ], recv_sem.at[7])
        lane, row = iota((NZ, 16, 128), 2), iota((NZ, 16, 128), 1)
        peak = jnp.sum(jnp.where(lane == row, zstat[...], 0.0), axis=2, keepdims=True)
        total = jnp.sum(jnp.where(lane == row + 16, zstat[...], 0.0), axis=2, keepdims=True)
        factor = jnp.exp(peak - jnp.max(peak, axis=0, keepdims=True))
        part = jnp.sum(factor * zrecv[...].astype(F32), axis=0)
        final[...] = (part / jnp.sum(factor * total, axis=0)).astype(BF)
        remote(final, final, 8, ((z + 8) * NXY + xy, head))

    @pl.when(z >= 8)
    def _():
        took(final, recv_sem.at[8])

    attention = final[...]
    row = iota((64, 16), 0)
    pick = row // 16 * 4 + row % 4 == iota((64, 16), 1)
    spread = dot(jnp.where(pick, 1.0, 0.0).astype(BF), attention).astype(BF)
    lined = jnp.concatenate([spread[h * 16 : (h + 1) * 16] for h in range(LOCAL)], axis=1)
    loads["wo"].wait()
    hidden = dot(lined, wo[...])
    block = iota((16, 128), 0) // 4
    for j in range(4):
        tile = jnp.zeros((16, 128), F32)
        for c in range(4):
            at = j * 512 + c * 128
            tile = jnp.where(block == c, hidden[:, at : at + 128], tile)
        psend[j] = tile.astype(BF)
    precv[0] = psend[head]

    for turn in (2, 1, 3, 0):
        there = (head + turn) % 4

        def send_plane(j, carry, turn=turn, there=there):
            rel = (j + 6) % NXY if turn else NXY - 1 - j
            slot = back(rel) * 4 + (4 - turn) % 4
            remote(psend.at[there], precv.at[slot], 5, (xy_device(rel), there))
            return carry

        lax.fori_loop(0, NXY if turn else NXY - 1, send_plane, 0)

    took(grecv.at[1:NXY], recv_sem.at[4])
    stats = grecv[:, :, LAT:].astype(F32)
    blocks = []
    for h in range(LOCAL):
        got = grecv[:, :, h * 128 : (h + 1) * 128].astype(F32)
        peak, total, part = merge(stats, 8 * h, got)
        blocks.append((part / total).astype(BF))
    hidden = dot(jnp.concatenate(blocks, axis=1), wo[...]).astype(BF)
    for j in range(4):
        hsend[j] = hidden[:, j * 512 : (j + 1) * 512]
    hrecv[0] = hsend[head]
    for turn in (2, 3, 1):
        there = (head + turn) % 4
        remote(hsend.at[there], hrecv.at[4 - turn], 6, (ctx, there))

    took(precv.at[1:32], recv_sem.at[5])
    summed = jnp.sum(precv[...].astype(F32).reshape(NXY, 4, 16, 128), axis=1)
    summed = summed.reshape(128, 128).astype(BF)
    row = iota((128, 128), 0)
    col = iota((128, 128), 1)
    pick = (row // 32 == col // 4 % 4) & (row % 32 == absolute(col // 16) * 4 + col % 4)
    placed = dot(jnp.where(pick, 1.0, 0.0).astype(BF), summed)
    decode_out[...] = (
        jnp.concatenate([placed[c * 32 : (c + 1) * 32] for c in range(4)], axis=1)
        .reshape(2, 2, 8, 512)
        .astype(BF)
    )
    took(hrecv.at[1:4], recv_sem.at[6])
    group_out[...] = (
        jnp.sum(hrecv[...].astype(F32), axis=0).reshape(2, 8, 512).astype(BF)
    )

    for phase, ref in (
        (2, queries.at[1:NXY]), (3, drecv.at[1:NXY]),
        (4, grecv.at[1:NXY]), (5, precv.at[1:32]), (6, hrecv.at[1:4]),
    ):
        took(ref, send_sem.at[phase])

    on_core(lambda keys: took(keys.at[1:NZ], send_sem.at[0]))

    @pl.when(z < 8)
    def _():
        took(zrecv.at[1:8], send_sem.at[1])
        took(zstat.at[1:8], send_sem.at[7])
        took(final, send_sem.at[8])

    @pl.when(z >= 8)
    def _():
        took(zrecv.at[1:9], send_sem.at[1])
        took(zstat.at[1:9], send_sem.at[7])

    def sent_keys(distance, carry):
        on_core(lambda keys: took(keys.at[1], key_send.at[distance]))
        return carry

    lax.fori_loop(1, NZ - z, sent_keys, 0)


def shards(
    cache_latent, group_latent, group_query, decode_query, group_start, w_key, w_value, w_out
):
    hbm = pl.BlockSpec(memory_space=pltpu.HBM)
    vmem = pl.BlockSpec(memory_space=pltpu.VMEM)
    return pl.pallas_call(
        kernel,
        out_shape=(
            jax.ShapeDtypeStruct((2, 8, 512), BF),
            jax.ShapeDtypeStruct((2, 2, 8, 512), BF),
        ),
        in_specs=[hbm] * 8,
        out_specs=(vmem, vmem),
        scratch_shapes=[
            pltpu.SMEM((2,), jnp.int32),
            pltpu.VMEM((2, 576, 256), BF),
            pltpu.VMEM((2, 8, 576), BF),
            pltpu.VMEM((2, 8, 768), BF),
            pltpu.VMEM((2, 2, 8, 768), BF),
            pltpu.VMEM((512, 512), BF),
            pltpu.VMEM((512, 512), BF),
            pltpu.VMEM((512, 2048), BF),
            pltpu.VMEM((NZ, 16, SPLIT), BF),
            pltpu.VMEM((NZ, 16, PADDED - SPLIT), BF),
            pltpu.VMEM((NXY, 16, 768), BF),
            pltpu.VMEM((512, PADDED), BF),
            pltpu.VMEM((NXY, 16, 256), BF),
            pltpu.VMEM((NXY, 16, 256), BF),
            pltpu.VMEM((NZ, 16, 128), BF),
            pltpu.VMEM((NZ, 1, 128), F32),
            pltpu.VMEM((16, 128), BF),
            pltpu.VMEM((4, 16, 128), BF),
            pltpu.VMEM((32, 16, 128), BF),
            pltpu.VMEM((NXY, 16, 640), BF),
            pltpu.VMEM((NXY, 16, 640), BF),
            pltpu.VMEM((4, 16, 512), BF),
            pltpu.VMEM((4, 16, 512), BF),
            pltpu.SemaphoreType.DMA((8,)),
            pltpu.SemaphoreType.DMA((9,)),
            pltpu.SemaphoreType.DMA((9,)),
            pltpu.SemaphoreType.DMA((NZ,)),
            pltpu.SemaphoreType.DMA((NZ,)),
            pltpu.SemaphoreType.REGULAR((NZ,)),
        ],
        compiler_params=pltpu.CompilerParams(
            collective_id=0, has_side_effects=True, vmem_limit_bytes=32 << 20
        ),
        name="latent_attention",
    )(
        *(
            pltpu.with_memory_space_constraint(array, pltpu.HBM)
            for array in (
                group_start, cache_latent.transpose(0, 2, 1), group_latent, group_query,
                decode_query, w_key, w_value, w_out,
            )
        )
    )


def solution(mesh):
    in_specs = (
        P(None, "ctx", None),
        P(None, "ctx", None),
        P(None, "ctx", "head"),
        P(None, None, None, "head"),
        P(),
        P(None, "head"),
        P(None, "head"),
        P("head", None),
    )
    out_specs = (P(None, "ctx", "head"), P(None, None, None, "head"))
    return jax.shard_map(shards, mesh=mesh, in_specs=in_specs, out_specs=out_specs, check_vma=False)
```

```python
import jax
import jax.numpy as jnp
from jax import lax
from jax.experimental import pallas as pl
from jax.experimental.pallas import tpu as pltpu
from jax.sharding import PartitionSpec as P

MESH = pl.DeviceIdType.MESH
BF = jnp.bfloat16
F32 = jnp.float32
LAT = 512
ROPE = 64
NOPE = 128
WIDE = NOPE + ROPE
PADDED = 640
SPLIT = 256
LOCAL = 4
NZ = 16
NXY = 8
SCALE = 1.0 / WIDE**0.5
LOW = -1e30


def dot(a, b):
    return lax.dot_general(a, b, (((1,), (0,)), ((), ())), preferred_element_type=F32)


def dot_t(a, b):
    return lax.dot_general(a, b, (((1,), (1,)), ((), ())), preferred_element_type=F32)


def iota(shape, axis):
    return lax.broadcasted_iota(jnp.int32, shape, axis)


def split(value, pieces):
    out = []
    for _ in range(pieces):
        head = value.astype(BF).astype(F32)
        out.append(head)
        value = value - head
    return out


def by_lane(shape, columns):
    lane = iota(shape, 1)
    tile = jnp.zeros(shape, F32)
    for at, column in columns.items():
        tile = jnp.where(lane == at, column, tile)
    return tile


def merge(stats, at, blocks):
    peak = stats[..., at : at + 1] + stats[..., at + 1 : at + 2] + stats[..., at + 2 : at + 3]
    total = stats[..., at + 3 : at + 4] + stats[..., at + 4 : at + 5]
    top = jnp.max(peak, axis=0, keepdims=True)
    factor = jnp.exp(peak - top)
    return top[0], jnp.sum(factor * total, axis=0), jnp.sum(factor * blocks, axis=0)


def kernel(
    start_hbm, cache_hbm, glat_hbm, gq_hbm, dq_hbm, wk_hbm, wv_hbm, wo_hbm,
    group_out, decode_out,
    start, cache, glat, gq, dq, wk, wv, wo,
    keys_a, keys_b, queries, big_q, dsend, drecv, zrecv, zstat, final, psend, precv,
    gsend, grecv, hsend, hrecv,
    local_sem, send_sem, recv_sem, key_send, key_recv, here,
):
    ctx = lax.axis_index("ctx")
    head = lax.axis_index("head")
    z = ctx // NXY
    xy = ctx % NXY
    yl = xy // 4
    x = xy % 4
    core = head % 2
    sibling = head // 2 * 2 + (1 - core)

    def xy_device(rel):
        dy, dx = rel // 4, rel % 4
        return z * NXY + (yl + dy) % 2 * 4 + (x + dx) % 4

    def back(rel):
        return rel // 4 * 4 + (4 - rel % 4) % 4

    def z_device(d):
        return (z + d) % NZ * NXY + xy

    def absolute(rel):
        return (yl + rel // 4) % 2 * 4 + (x + rel % 4) % 4

    def remote(src, dst, phase, device):
        pltpu.make_async_remote_copy(
            src_ref=src, dst_ref=dst, send_sem=send_sem.at[phase], recv_sem=recv_sem.at[phase],
            device_id=device, device_id_type=MESH,
        ).start()

    def took(ref, sem):
        pltpu.make_async_copy(ref, ref, sem).wait()

    loads = {}
    for at, (name, src, dst) in enumerate((
        ("glat", glat_hbm, glat), ("gq", gq_hbm, gq), ("dq", dq_hbm, dq), ("wk", wk_hbm, wk),
        ("start", start_hbm, start), ("cache", cache_hbm, cache), ("wv", wv_hbm, wv),
        ("wo", wo_hbm, wo),
    )):
        loads[name] = pltpu.make_async_copy(src, dst, local_sem.at[at])
        if name != "wo":
            loads[name].start()
    keys_a[...] = jnp.zeros_like(keys_a)
    keys_b[...] = jnp.zeros_like(keys_b)
    barrier = pltpu.get_barrier_semaphore()

    def greet(device):
        pl.semaphore_signal(barrier, inc=1, device_id=device, device_id_type=MESH)

    def ranked(r):
        return jnp.where(r < 6, r, jnp.where(r < 10, r + 6, r - 4))

    def rank_of(there):
        return jnp.where(there < 6, there, jnp.where(there < 12, there + 4, there - 6))

    rank = rank_of(z)

    def greet_z(r, carry):
        greet((ranked(r) * NXY + xy, head))
        return carry

    lax.fori_loop(rank + 1, NZ, greet_z, 0)
    for rel in range(1, NXY):
        greet((xy_device(rel), head))
    for rel in range(1, 4):
        greet((ctx, (head + rel) % 4))

    loads["glat"].wait()
    own = glat[...].astype(F32).reshape(16, LAT + ROPE).astype(BF)
    keys_a[0] = own[:, :SPLIT]
    keys_b[0] = jnp.concatenate([own[:, SPLIT:], jnp.zeros((16, PADDED - LAT - ROPE), BF)], axis=1)

    def on_core(action):
        for at, keys in enumerate((keys_a, keys_b)):

            @pl.when(core == at)
            def _(keys=keys):
                action(keys)

    def send_keys(there):
        on_core(
            lambda keys: pltpu.make_async_remote_copy(
                src_ref=keys.at[0], dst_ref=keys.at[there - z],
                send_sem=key_send.at[there - z], recv_sem=key_recv.at[there - z],
                device_id=(there * NXY + xy, head), device_id_type=MESH,
            ).start()
        )

    def to_lower(r, carry):
        there = ranked(r)

        @pl.when((there > z) & (z < 8))
        def _():
            send_keys(there)

        @pl.when(there < z)
        def _():
            pl.semaphore_signal(
                here.at[z], inc=1, device_id=(there * NXY + xy, head), device_id_type=MESH
            )

        return carry

    def send_z(there):
        slot = (z - there + NZ) % NZ
        remote(zrecv.at[0], zrecv.at[slot], 1, (there * NXY + xy, head))
        remote(zstat.at[0], zstat.at[slot], 7, (there * NXY + xy, head))

    def part_to_lower(r, carry):
        send_z(r)
        return carry

    def ahead(j):
        return (z + (j + 1) // 2 * (2 * (j % 2) - 1) + NZ) % NZ

    def keys_to_higher(j, carry):
        there = ahead(j)

        @pl.when((there > z + 3) & (rank_of(there) > rank))
        def _():
            pl.semaphore_wait(here.at[there], 1)
            send_keys(there)

        return carry

    def keys_direct(there, carry):
        send_keys(there)
        return carry

    def part_to_higher(j, carry):
        there = ahead(j)

        @pl.when((there > z) & (there < 8))
        def _():
            send_z(there)

        return carry

    def keys_to_next(there, carry):
        @pl.when(rank_of(there) > rank)
        def _():
            pl.semaphore_wait(here.at[there], 1)
            send_keys(there)

        return carry

    def from_lower(there, carry):
        @pl.when((z < 12) | (there // 2 != 3))
        def _():
            on_core(lambda keys: took(keys.at[1], key_recv.at[z - there]))

        return carry

    loads["dq"].wait()
    rows = NXY * 16
    flat = dq[...].astype(F32).reshape(32, LOCAL * WIDE).astype(BF)
    row = iota((rows, 32), 0)
    pick = absolute(row // 16) * 4 + row % 4 == iota((rows, 32), 1)
    spread = dot(jnp.where(pick, 1.0, 0.0).astype(BF), flat)
    row = iota((rows, 1), 0)
    row_head = row // 4 % 4
    row_req = absolute(row // 16) // 2 % 2
    nope = jnp.concatenate(
        [
            jnp.where(row_head == h, spread[:, h * WIDE : h * WIDE + NOPE], 0.0)
            for h in range(LOCAL)
        ],
        axis=1,
    ).astype(BF)
    rope = jnp.zeros((rows, ROPE), F32)
    for h in range(LOCAL):
        rope = jnp.where(row_head == h, spread[:, h * WIDE + NOPE : (h + 1) * WIDE], rope)
    rope = rope.astype(BF)
    loads["wk"].wait()
    absorbed = dot_t(nope, wk[...]).astype(BF)

    loads["start"].wait()
    loads["cache"].wait()
    scores = []
    masks = []
    for r in range(2):
        got = dot(absorbed, cache[r, :LAT]) + dot(rope, cache[r, LAT:])
        position = ctx * 256 + iota((1, 256), 1)
        allowed = (position < start[r]) & (row_req == r)
        masks.append(allowed)
        scores.append(jnp.where(allowed, got * SCALE, LOW))
    got = dot_t(absorbed, own[:, :LAT]) + dot_t(rope, own[:, LAT:])
    allowed = iota((1, 16), 1) // 8 == row_req
    masks.append(allowed)
    scores.append(jnp.where(allowed, got * SCALE, LOW))
    peak = jnp.max(scores[0], axis=1, keepdims=True)
    for got in scores[1:]:
        peak = jnp.maximum(peak, jnp.max(got, axis=1, keepdims=True))
    total = jnp.zeros((rows, 1), F32)
    mixture = jnp.zeros((rows, LAT), F32)
    for k, (got, allowed) in enumerate(zip(scores, masks)):
        weights = jnp.where(allowed, jnp.exp(got - peak), 0.0)
        total = total + jnp.sum(weights, axis=1, keepdims=True)
        weights = weights.astype(BF)
        mixture = mixture + (
            dot_t(weights, cache[k, :LAT]) if k < 2 else dot(weights, own[:, :LAT])
        )
    loads["wv"].wait()
    wide = dot(mixture.astype(BF), wv[...])
    part = jnp.zeros((rows, NOPE), F32)
    for h in range(LOCAL):
        part = jnp.where(row_head == h, wide[:, h * 128 : (h + 1) * 128], part)
    stats = by_lane((rows, 128), dict(enumerate(split(peak, 3) + split(total, 2))))
    packed = jnp.concatenate([part, stats], axis=1).astype(BF).reshape(NXY, 16, 256)
    dsend[...] = packed
    drecv[0] = packed[0]
    pl.semaphore_wait(barrier, 10 + rank)
    for rel in (6, 2, 5, 7, 4, 1, 3):
        remote(dsend.at[rel], drecv.at[back(rel)], 3, (xy_device(rel), head))

    lax.fori_loop(0, rank, to_lower, 0)
    loads["gq"].wait()
    queries[0] = gq[...].astype(F32).reshape(16, LOCAL * WIDE).astype(BF)
    for rel in (6, 2, 5, 7, 4, 1, 3):
        remote(queries.at[0], queries.at[back(rel)], 2, (xy_device(rel), head))

    loads["wo"].start()

    lax.fori_loop(z + 1, jnp.minimum(z + 4, NZ), keys_to_next, 0)

    took(drecv.at[1:NXY], recv_sem.at[3])
    packed = drecv[...].astype(F32)
    peak, total, part = merge(packed[..., 128:], 0, packed[..., :128])
    zrecv[0] = part.astype(BF)
    lane, row = iota((16, 128), 1), iota((16, 128), 0)
    zstat[0] = jnp.sum(
        jnp.where(lane == row, peak, jnp.where(lane == row + 16, total, 0.0)),
        axis=0, keepdims=True,
    )

    lax.fori_loop(0, jnp.where(z < 12, jnp.minimum(z, 8), 6), part_to_lower, 0)
    @pl.when(z // 4 == 2)
    def _():
        lax.fori_loop(12, NZ, keys_direct, 0)

    lax.fori_loop(1, NZ, keys_to_higher, 0)
    lax.fori_loop(1, NZ, part_to_higher, 0)

    @pl.when(z >= 12)
    def _():
        for there in (7, 6):
            on_core(lambda keys, there=there: took(keys.at[1], key_recv.at[z - there]))
            send_z(there)


    took(queries.at[1:NXY], recv_sem.at[2])
    all_q = queries[...].reshape(128, LOCAL * WIDE)
    for h in range(LOCAL):
        block = dot_t(all_q[:, h * WIDE : h * WIDE + NOPE], wk[:, h * 128 : (h + 1) * 128])
        big_q[h * 128 : (h + 1) * 128, :LAT] = block.astype(BF)
        big_q[h * 128 : (h + 1) * 128, LAT:] = jnp.concatenate(
            [
                all_q[:, h * WIDE + NOPE : (h + 1) * WIDE],
                jnp.zeros((128, PADDED - LAT - ROPE), BF),
            ],
            axis=1,
        )

    lax.fori_loop(0, z, from_lower, 0)
    on_core(lambda keys: remote(keys.at[1:NZ], keys.at[1:NZ], 0, (ctx, sibling)))
    for at, keys in enumerate((keys_b, keys_a)):

        @pl.when(core == at)
        def _(keys=keys):
            took(keys.at[1:NZ], recv_sem.at[0])


    first = keys_a[...].reshape(256, SPLIT)
    second = keys_b[...].reshape(256, PADDED - SPLIT)
    scores = dot_t(big_q[:, :SPLIT], first) + dot_t(big_q[:, SPLIT:], second)
    row = iota((LOCAL * 128, 1), 0)
    col = iota((1, 256), 1)
    query_at = (z * NXY + absolute(row // 16 % NXY)) * 8 + row % 8
    key_z = z - col // 16
    key_at = (key_z * NXY + xy) * 8 + col % 8
    allowed = (key_z >= 0) & (key_at <= query_at) & (row // 8 % 2 == col // 8 % 2)
    scores = jnp.where(allowed, scores * SCALE, LOW)
    peak = jnp.max(scores, axis=1, keepdims=True)
    weights = jnp.where(allowed, jnp.exp(scores - peak), 0.0)
    total = jnp.sum(weights, axis=1, keepdims=True)
    weights = weights.astype(BF)
    mixture = jnp.concatenate(
        [dot(weights, first), dot(weights, second[:, : LAT - SPLIT])], axis=1
    ).astype(BF)
    columns = {}
    for h in range(LOCAL):
        at = slice(h * 128, (h + 1) * 128)
        part = dot(mixture[at], wv[:, at]).astype(BF).reshape(NXY, 16, 128)
        gsend[:, :, at] = part
        grecv[0, :, at] = part[0]
        for k, column in enumerate(split(peak[at], 3) + split(total[at], 2)):
            columns[8 * h + k] = column
    stats = by_lane((128, 128), columns).astype(BF).reshape(NXY, 16, 128)
    gsend[:, :, LAT:] = stats
    grecv[0, :, LAT:] = stats[0]
    for rel in (6, 2, 5, 7, 4, 1, 3):
        remote(gsend.at[rel], grecv.at[back(rel)], 4, (xy_device(rel), head))

    @pl.when(z < 8)
    def _():
        took(zrecv.at[1:NZ], recv_sem.at[1])
        took(zstat.at[1:NZ], recv_sem.at[7])
        lane, row = iota((NZ, 16, 128), 2), iota((NZ, 16, 128), 1)
        peak = jnp.sum(jnp.where(lane == row, zstat[...], 0.0), axis=2, keepdims=True)
        total = jnp.sum(jnp.where(lane == row + 16, zstat[...], 0.0), axis=2, keepdims=True)
        factor = jnp.exp(peak - jnp.max(peak, axis=0, keepdims=True))
        part = jnp.sum(factor * zrecv[...].astype(F32), axis=0)
        final[...] = (part / jnp.sum(factor * total, axis=0)).astype(BF)
        remote(final, final, 8, ((z + 8) * NXY + xy, head))

    @pl.when(z >= 8)
    def _():
        took(final, recv_sem.at[8])

    attention = final[...]
    row = iota((64, 16), 0)
    pick = row // 16 * 4 + row % 4 == iota((64, 16), 1)
    spread = dot(jnp.where(pick, 1.0, 0.0).astype(BF), attention).astype(BF)
    lined = jnp.concatenate([spread[h * 16 : (h + 1) * 16] for h in range(LOCAL)], axis=1)
    loads["wo"].wait()
    hidden = dot(lined, wo[...])
    block = iota((16, 128), 0) // 4
    for j in range(4):
        tile = jnp.zeros((16, 128), F32)
        for c in range(4):
            at = j * 512 + c * 128
            tile = jnp.where(block == c, hidden[:, at : at + 128], tile)
        psend[j] = tile.astype(BF)
    precv[0] = psend[head]

    for turn in (2, 1, 3, 0):
        there = (head + turn) % 4

        def send_plane(j, carry, turn=turn, there=there):
            rel = (j + 6) % NXY if turn else NXY - 1 - j
            slot = back(rel) * 4 + (4 - turn) % 4
            remote(psend.at[there], precv.at[slot], 5, (xy_device(rel), there))
            return carry

        lax.fori_loop(0, NXY if turn else NXY - 1, send_plane, 0)

    took(grecv.at[1:NXY], recv_sem.at[4])
    stats = grecv[:, :, LAT:].astype(F32)
    blocks = []
    for h in range(LOCAL):
        got = grecv[:, :, h * 128 : (h + 1) * 128].astype(F32)
        peak, total, part = merge(stats, 8 * h, got)
        blocks.append((part / total).astype(BF))
    hidden = dot(jnp.concatenate(blocks, axis=1), wo[...]).astype(BF)
    for j in range(4):
        hsend[j] = hidden[:, j * 512 : (j + 1) * 512]
    hrecv[0] = hsend[head]
    for turn in (2, 3, 1):
        there = (head + turn) % 4
        remote(hsend.at[there], hrecv.at[4 - turn], 6, (ctx, there))

    took(precv.at[1:32], recv_sem.at[5])
    summed = jnp.sum(precv[...].astype(F32).reshape(NXY, 4, 16, 128), axis=1)
    summed = summed.reshape(128, 128).astype(BF)
    row = iota((128, 128), 0)
    col = iota((128, 128), 1)
    pick = (row // 32 == col // 4 % 4) & (row % 32 == absolute(col // 16) * 4 + col % 4)
    placed = dot(jnp.where(pick, 1.0, 0.0).astype(BF), summed)
    decode_out[...] = (
        jnp.concatenate([placed[c * 32 : (c + 1) * 32] for c in range(4)], axis=1)
        .reshape(2, 2, 8, 512)
        .astype(BF)
    )
    took(hrecv.at[1:4], recv_sem.at[6])
    group_out[...] = (
        jnp.sum(hrecv[...].astype(F32), axis=0).reshape(2, 8, 512).astype(BF)
    )

    for phase, ref in (
        (2, queries.at[1:NXY]), (3, drecv.at[1:NXY]),
        (4, grecv.at[1:NXY]), (5, precv.at[1:32]), (6, hrecv.at[1:4]),
    ):
        took(ref, send_sem.at[phase])

    on_core(lambda keys: took(keys.at[1:NZ], send_sem.at[0]))

    @pl.when(z < 8)
    def _():
        took(zrecv.at[1:8], send_sem.at[1])
        took(zstat.at[1:8], send_sem.at[7])
        took(final, send_sem.at[8])

    @pl.when(z >= 8)
    def _():
        took(zrecv.at[1:9], send_sem.at[1])
        took(zstat.at[1:9], send_sem.at[7])

    def sent_keys(distance, carry):
        on_core(lambda keys: took(keys.at[1], key_send.at[distance]))
        return carry

    lax.fori_loop(1, NZ - z, sent_keys, 0)


def shards(
    cache_latent, group_latent, group_query, decode_query, group_start, w_key, w_value, w_out
):
    hbm = pl.BlockSpec(memory_space=pltpu.HBM)
    vmem = pl.BlockSpec(memory_space=pltpu.VMEM)
    return pl.pallas_call(
        kernel,
        out_shape=(
            jax.ShapeDtypeStruct((2, 8, 512), BF),
            jax.ShapeDtypeStruct((2, 2, 8, 512), BF),
        ),
        in_specs=[hbm] * 8,
        out_specs=(vmem, vmem),
        scratch_shapes=[
            pltpu.SMEM((2,), jnp.int32),
            pltpu.VMEM((2, 576, 256), BF),
            pltpu.VMEM((2, 8, 576), BF),
            pltpu.VMEM((2, 8, 768), BF),
            pltpu.VMEM((2, 2, 8, 768), BF),
            pltpu.VMEM((512, 512), BF),
            pltpu.VMEM((512, 512), BF),
            pltpu.VMEM((512, 2048), BF),
            pltpu.VMEM((NZ, 16, SPLIT), BF),
            pltpu.VMEM((NZ, 16, PADDED - SPLIT), BF),
            pltpu.VMEM((NXY, 16, 768), BF),
            pltpu.VMEM((512, PADDED), BF),
            pltpu.VMEM((NXY, 16, 256), BF),
            pltpu.VMEM((NXY, 16, 256), BF),
            pltpu.VMEM((NZ, 16, 128), BF),
            pltpu.VMEM((NZ, 1, 128), F32),
            pltpu.VMEM((16, 128), BF),
            pltpu.VMEM((4, 16, 128), BF),
            pltpu.VMEM((32, 16, 128), BF),
            pltpu.VMEM((NXY, 16, 640), BF),
            pltpu.VMEM((NXY, 16, 640), BF),
            pltpu.VMEM((4, 16, 512), BF),
            pltpu.VMEM((4, 16, 512), BF),
            pltpu.SemaphoreType.DMA((8,)),
            pltpu.SemaphoreType.DMA((9,)),
            pltpu.SemaphoreType.DMA((9,)),
            pltpu.SemaphoreType.DMA((NZ,)),
            pltpu.SemaphoreType.DMA((NZ,)),
            pltpu.SemaphoreType.REGULAR((NZ,)),
        ],
        compiler_params=pltpu.CompilerParams(
            collective_id=0, has_side_effects=True, vmem_limit_bytes=32 << 20
        ),
        name="latent_attention",
    )(
        *(
            pltpu.with_memory_space_constraint(array, pltpu.HBM)
            for array in (
                group_start, cache_latent.transpose(0, 2, 1), group_latent, group_query,
                decode_query, w_key, w_value, w_out,
            )
        )
    )


def solution(mesh):
    in_specs = (
        P(None, "ctx", None),
        P(None, "ctx", None),
        P(None, "ctx", "head"),
        P(None, None, None, "head"),
        P(),
        P(None, "head"),
        P(None, "head"),
        P("head", None),
    )
    out_specs = (P(None, "ctx", "head"), P(None, None, None, "head"))
    return jax.shard_map(shards, mesh=mesh, in_specs=in_specs, out_specs=out_specs, check_vma=False)
```
